32 devices in a mesh: section: 16 (over z, y, x), tp: 2 (over core).
Axes of the slice: x: 2, y: 2, z: 4, core: 2. Of those that a mesh axis runs over, the one named last changes fastest.
Arguments:
- hidden_t: bfloat16 [8192, 384], P('tp'), may hold values from -40 to 40
- norm_gain: bfloat16 [4, 8192], replicated, may hold values from 0.099609375 to 1.8984375
- q_weight: bfloat16 [16, 8192, 512], P('section', None, 'tp'), may hold values from -0.0625 to 0.0625
- k_weight: bfloat16 [16, 2048, 256], P('section', None, 'tp'), may hold values from -0.0625 to 0.0625
- v_weight: bfloat16 [16, 2048, 256], P('section', None, 'tp'), may hold values from -0.0625 to 0.0625
- o_weight: bfloat16 [16, 512, 8192], P('section', 'tp'), may hold values from -0.125 to 0.125
- lengths: int32 [16], replicated, may hold values from 1 to 48, 384 in all
- prior_offsets: int32 [16], replicated, may hold values from 0 to 4095
- owners: int32 [16], replicated, may hold values from 0 to 15, each once
Outputs:
- final_hidden: bfloat16 [8192, 384], P('tp', 'section')
- kv_cache: bfloat16 [16, 4, 48, 512], P('section', None, None, 'tp')
The draws below stay inside these ranges and needn't reach their ends.
Inputs may be any that keep to these rules, and one draw needn't show every extreme that they name: `lengths`: the 16 requests fill all 384 tokens; some request has exactly 48 tokens. `owners`: each owner serves exactly one request.
All inputs are finite; a program needn't handle non-finite values.
Results may differ from the reference program's by a relative error of at most 0.023.
Values may be sent and summed in bfloat16 or wider, within the bound.
A program may use at most 128 MiB of HBM per device.

```python
import math
import jax
import jax.numpy as jnp
import numpy as np
from jax import lax

D = 8192
HEAD_DIM = 128
QPG = 8
SUBS = 4
TOKENS = 384
MAXPOS = 4096
QSUB = 2
KV_HEADS = 2
LAYERS = 4
REQS = 16
CAP = 48


def draw_hidden_t(key, part):
    key = jax.random.fold_in(key, 7)
    key_base, key_cols = jax.random.split(key, 2)
    col_scale = jnp.exp(jax.random.uniform(key_cols, (1, TOKENS), jnp.float32, 0.0, math.log(10.0)))
    base_vals = jnp.clip(jax.random.normal(key_base, (D, TOKENS), jnp.float32), -4.0, 4.0)
    return (base_vals * col_scale).astype(jnp.bfloat16)


def place_ends(array, own_key, least, largest):
    place = [jax.random.randint(jax.random.fold_in(own_key, axis), (), 0, length) for axis, length in enumerate(array.shape)]
    longest = array.shape.index(max(array.shape))
    neighbour = place[:longest] + [(place[longest] + 1) % array.shape[longest]] + place[longest + 1:]
    return array.at[tuple(place)].set(least).at[tuple(neighbour)].set(largest)


def steps_of(own_key, shape, cuts, least, high):
    gain = 1.0
    for axis_at, blocks in cuts:
        heights = jax.random.uniform(jax.random.fold_in(jax.random.fold_in(own_key, 6), axis_at), (blocks,), jnp.float32, least / len(cuts), high / len(cuts))
        gain = gain * jnp.repeat(jnp.exp(heights), shape[axis_at] // blocks).reshape((-1,) + (1,) * (len(shape) - 1 - axis_at))
    return gain


def profile(number_of, total, reach, slope):
    loads = [(1 << 20) // math.isqrt(rank ** slope) + 1 for rank in range(2, number_of + 1)]
    rest, holding = total - reach - (number_of - 1), [1] * (number_of - 1)
    while rest > 0:
        movable = [i for i in range(number_of - 1) if holding[i] < reach]
        mass, remaining = sum([loads[i] for i in movable]), rest
        for i in movable:
            extra = min(reach - holding[i], max(1, remaining * loads[i] // mass), rest)
            holding[i] = holding[i] + extra
            rest = rest - extra
    return np.array([reach] + holding)


def ragged(stream_key, count, total, reach, slope):
    if count == 2:
        one = jax.random.randint(stream_key, (), max(1, total - reach), min(reach, total - 1) + 1)
        return jnp.stack([one, total - one])
    sizes = jnp.asarray(profile(count, total, reach, slope), jnp.int32)
    twos = (count - 1) // 2
    giver, receiver = sizes[1:1 + 2 * twos:2], sizes[2:2 + 2 * twos:2]
    room = jnp.minimum(giver - 1, reach - receiver)
    shifted = jax.random.randint(jax.random.fold_in(stream_key, 1), (twos,), 0, 1 << 20) % (room + 1)
    sizes = sizes.at[1:1 + 2 * twos:2].set(giver - shifted).at[2:2 + 2 * twos:2].set(receiver + shifted)
    return sizes[jax.random.permutation(jax.random.fold_in(stream_key, 2), count)]


def centred(rng, shape, scale, reach, pieces=(), held_as=jnp.bfloat16):
    loudness = steps_of(rng, shape, pieces, -0.22, 0.18) if pieces else 1.0
    array = jax.random.normal(rng, shape, jnp.float32) * scale * loudness
    return jnp.minimum(jnp.maximum(array, -reach), reach).astype(held_as)


def setup_inputs(seed: int = 0) -> dict:
    arg_keys = jax.random.split(jax.random.key(seed), 10)
    hidden_t = draw_hidden_t(jax.random.fold_in(arg_keys[9], 71), 0)
    norm_gain = jnp.clip(1.0 + 0.18 * jax.random.normal(arg_keys[1], (LAYERS, D), jnp.float32), 0.099609375, 1.8984375).astype(jnp.bfloat16)
    q_weight = centred(arg_keys[2], (LAYERS * SUBS, D, KV_HEADS * QSUB * HEAD_DIM), D ** -0.5, 0.0625, ((0, 16), (2, 2)))
    k_weight = centred(arg_keys[3], (LAYERS * SUBS, D // SUBS, KV_HEADS * HEAD_DIM), D ** -0.5, 0.0625, ((0, 16), (2, 2)))
    v_weight = centred(arg_keys[4], (LAYERS * SUBS, D // SUBS, KV_HEADS * HEAD_DIM), D ** -0.5, 0.0625, ((0, 16), (2, 2)))
    o_weight = centred(arg_keys[5], (LAYERS * SUBS, KV_HEADS * QSUB * HEAD_DIM, D), (KV_HEADS * QPG * HEAD_DIM) ** -0.5, 0.125, ((0, 16), (1, 2)))
    lengths = ragged(arg_keys[6], REQS, TOKENS, CAP, 2).astype(jnp.int32)
    prior_offsets = place_ends(jax.random.randint(arg_keys[7], (REQS,), 0, MAXPOS), jax.random.fold_in(arg_keys[7], 1), 0, MAXPOS - 1).astype(jnp.int32)
    owners = jax.random.permutation(arg_keys[8], REQS).astype(jnp.int32)
    return dict(hidden_t=hidden_t, norm_gain=norm_gain, q_weight=q_weight, k_weight=k_weight, v_weight=v_weight, o_weight=o_weight, lengths=lengths, prior_offsets=prior_offsets, owners=owners)


NORM_EPS = 1e-05
ROPE_BASE = 500000.0

def rope_tables(positions):
    half_dim = HEAD_DIM // 2
    steps_i = jnp.arange(half_dim, dtype=jnp.float32)
    inv_freq = jnp.power(jnp.float32(ROPE_BASE), -(2.0 * steps_i) / HEAD_DIM)
    angle = positions.astype(jnp.float32)[:, None] * inv_freq[None, :]
    return (jnp.cos(angle)[:, None, :], jnp.sin(angle)[:, None, :])

def rotate_pairs(values, cos_table, sin_table):
    half_dim = values.shape[-1] // 2
    first_half = values[..., :half_dim]
    second_half = values[..., half_dim:]
    return jnp.concatenate([first_half * cos_table - second_half * sin_table, second_half * cos_table + first_half * sin_table], axis=-1)

def reference(hidden_t, norm_gain, q_weight, k_weight, v_weight, o_weight, lengths, prior_offsets, owners):
    tokens = hidden_t.shape[1]
    num_reqs = lengths.shape[0]
    req_ends = jnp.cumsum(lengths).astype(jnp.int32)
    req_starts = (req_ends - lengths).astype(jnp.int32)
    tok_ids = jnp.arange(tokens, dtype=jnp.int32)
    req_of_tok = lax.optimization_barrier(jnp.sum((tok_ids[:, None] >= req_ends[None, :]).astype(jnp.int32), axis=1))
    req_onehot = req_of_tok[:, None] == jnp.arange(num_reqs, dtype=jnp.int32)[None, :]
    positions = lax.optimization_barrier(jnp.sum(jnp.where(req_onehot, (prior_offsets - req_starts)[None, :], 0), axis=1)).astype(jnp.int32) + tok_ids
    key_mask = (req_of_tok[:, None] == req_of_tok[None, :]) & (tok_ids[None, :] <= tok_ids[:, None])
    cos_table, sin_table = rope_tables(positions)
    q_full = q_weight.reshape(LAYERS, SUBS, D, KV_HEADS, QSUB, HEAD_DIM).transpose(0, 2, 3, 1, 4, 5).reshape(LAYERS, D, KV_HEADS * QPG * HEAD_DIM)
    k_full = k_weight.reshape(LAYERS, D, KV_HEADS * HEAD_DIM)
    v_full = v_weight.reshape(LAYERS, D, KV_HEADS * HEAD_DIM)
    o_full = o_weight.reshape(LAYERS, SUBS, KV_HEADS, QSUB, HEAD_DIM, D).transpose(0, 2, 1, 3, 4, 5).reshape(LAYERS, KV_HEADS * QPG * HEAD_DIM, D)

    def layer(h_now, weights):
        gain_row, w_query, w_key, w_value, w_out = weights
        h_float = h_now.astype(jnp.float32)
        mean_square = lax.optimization_barrier(jnp.mean(h_float * h_float, axis=0))
        normed = (h_float * lax.rsqrt(mean_square + NORM_EPS)[None, :] * gain_row.astype(jnp.float32)[:, None]).astype(jnp.bfloat16)
        query_rows = jnp.dot(normed.T, w_query, preferred_element_type=jnp.float32)
        key_rows = jnp.dot(normed.T, w_key, preferred_element_type=jnp.float32)
        value_rows = jnp.dot(normed.T, w_value, preferred_element_type=jnp.float32)
        query_rot = rotate_pairs(query_rows.reshape(tokens, KV_HEADS * QPG, HEAD_DIM), cos_table, sin_table).astype(jnp.bfloat16)
        key_rot = rotate_pairs(key_rows.reshape(tokens, KV_HEADS, HEAD_DIM), cos_table, sin_table).astype(jnp.bfloat16)
        value_new = value_rows.reshape(tokens, KV_HEADS, HEAD_DIM).astype(jnp.bfloat16)
        query_grp = query_rot.reshape(tokens, KV_HEADS, QPG, HEAD_DIM).astype(jnp.float32)
        scores = jnp.einsum('tjgh,sjh->jgts', query_grp, key_rot.astype(jnp.float32)) / math.sqrt(HEAD_DIM)
        exp_scores = jnp.where(key_mask[None, None], jnp.exp(scores), 0.0)
        probs = (exp_scores / lax.optimization_barrier(jnp.sum(exp_scores, axis=-1, keepdims=True))).astype(jnp.bfloat16)
        attended = jnp.einsum('jgts,sjh->tjgh', probs.astype(jnp.float32), value_new.astype(jnp.float32)).astype(jnp.bfloat16)
        attended = attended.reshape(tokens, KV_HEADS, SUBS, QSUB * HEAD_DIM)
        out_groups = w_out.reshape(KV_HEADS, SUBS, QSUB * HEAD_DIM, w_out.shape[1])
        parts = jnp.einsum('tjuq,juqd->judt', attended.astype(jnp.float32), out_groups.astype(jnp.float32)).astype(jnp.bfloat16)
        updated = (h_float + lax.optimization_barrier(jnp.sum(parts.astype(jnp.float32), axis=(0, 1)))).astype(jnp.bfloat16)
        layer_kv = jnp.concatenate([key_rot, value_new], axis=-1).reshape(tokens, KV_HEADS * 2 * HEAD_DIM)
        return (updated, layer_kv)
    final_hidden, all_kv = lax.scan(layer, hidden_t, (norm_gain, q_full, k_full, v_full, o_full))
    owner_onehot = owners[None, :] == jnp.arange(num_reqs, dtype=jnp.int32)[:, None]
    owner_starts = lax.optimization_barrier(jnp.sum(jnp.where(owner_onehot, req_starts[None, :], 0), axis=1))
    owner_lens = lax.optimization_barrier(jnp.sum(jnp.where(owner_onehot, lengths[None, :], 0), axis=1))
    slot_ids = jnp.arange(CAP, dtype=jnp.int32)
    row_index = jnp.minimum(owner_starts[:, None] + slot_ids[None, :], tokens - 1).astype(jnp.int32)
    row_valid = slot_ids[None, :] < owner_lens[:, None]
    picked = all_kv[:, row_index]
    picked = jnp.transpose(picked, (1, 0, 2, 3))
    kv_cache = jnp.where(row_valid[:, None, :, None], picked, jnp.zeros((), jnp.bfloat16))
    return (final_hidden, kv_cache)
```

```python
import functools
import math

import jax
import jax.numpy as jnp
from jax import lax
from jax.experimental import pallas as pl
from jax.experimental.pallas import tpu as pltpu
from jax.sharding import PartitionSpec as P

HEAD_DIM = 128
SUBS = 4
BLOCK = 256
LAG = 2
NORM_EPS = 1e-05
ROPE_BASE = 500000.0
MESH = pl.DeviceIdType.MESH
F32 = jnp.float32
BF16 = jnp.bfloat16


def dot(a, b):
    return jnp.dot(a, b, preferred_element_type=F32)


def round_up(count, unit):
    return (count + unit - 1) // unit * unit


def relay_kernel(
    layers, tps, own_tokens,
    hin, gain, wq, wk, wv, wo, cosf, sinf, mask, pick,
    fin_out, kv_out,
    hbuf, qacc, kvacc, sumsq, kvst, kvrecv, kvb, att,
    s1out, s1in, s1own, s2in, upd, totf, fst, fin, pickst, kvbuf,
    hs, fwd_s, ag_s, kvp_s, kvp_r, s1_s, s1_r, s2_s, s2_r, z_s, pk_s, pk_r, fin_s, fin_r,
):
    section = lax.axis_index("section")
    t = lax.axis_index("tp")
    layer = section // SUBS
    u = section % SUBS
    chunks = hbuf.shape[1]
    tokens = hbuf.shape[2]
    depth = hbuf.shape[0] * chunks * BLOCK
    own = u * tps + t
    sections = layers * SUBS
    last = layers - 1
    out_tp = own // SUBS
    out_slot = own % SUBS
    base = layer * SUBS

    def copy(src, dst, send, recv, sec, core):
        return pltpu.make_async_remote_copy(
            src_ref=src, dst_ref=dst, send_sem=send, recv_sem=recv,
            device_id=(sec, core), device_id_type=MESH,
        )

    def sub_at(r):
        return (u + r) % SUBS

    def tp_at(e):
        return (t + e) % tps

    def first_copy(j, ci, e):
        p = t * SUBS + j
        return copy(hin.at[j, ci], hbuf.at[p, ci], fwd_s.at[j, ci, e - 1], hs.at[p, ci], section, tp_at(e))

    def fwd_copy(r, ci, e):
        p = sub_at(r) * tps + t
        return copy(hbuf.at[p, ci], hbuf.at[p, ci], fwd_s.at[r, ci, e - 1], hs.at[p, ci], section, tp_at(e))

    def ag_copy(r, ci):
        return copy(hbuf.at[own, ci], hbuf.at[own, ci], ag_s.at[r - 1, ci], hs.at[own, ci], base + sub_at(r), t)

    def wait_block(p, ci):
        copy(hbuf.at[p, ci], hbuf.at[p, ci], fwd_s.at[0, 0, 0], hs.at[p, ci], section, tp_at(1)).wait_recv()

    def kvp_copy(r):
        return copy(kvst, kvrecv.at[r - 1], kvp_s.at[r - 1], kvp_r.at[r - 1], base + sub_at(r), t)

    def s1_copy(r, ci, e):
        return copy(s1out.at[r, ci, e - 1], s1in.at[r, ci, e - 1], s1_s.at[r, ci, e - 1], s1_r.at[r, ci, e - 1],
                    section, tp_at(e))

    def s2_copy(r, ci):
        return copy(s1own.at[r, ci], s2in.at[r - 1, ci], s2_s.at[r - 1, ci], s2_r.at[r - 1, ci], base + sub_at(r), t)

    def z_copy(ci):
        return copy(upd.at[ci], hbuf.at[own, ci], z_s.at[ci], hs.at[own, ci], section + SUBS, t)

    def pick_copy(j):
        return copy(pickst.at[j], kvbuf.at[layer], pk_s.at[j], pk_r.at[layer], j * SUBS + u, t)

    def fin_copy(s):
        return copy(fst.at[s], fin.at[out_slot], fin_s.at[s], fin_r.at[out_slot], s, out_tp)

    def loop(count, body):
        def step(k, carry):
            body(k)
            return carry
        lax.fori_loop(0, count, step, jnp.int32(0))

    barrier = pltpu.get_barrier_semaphore()

    def greet(sec, core):
        pl.semaphore_signal(barrier, inc=1, device_id=(sec, core), device_id_type=MESH)

    for e in range(1, tps):
        greet(section, tp_at(e))
    for r in range(1, SUBS):
        greet(base + sub_at(r), t)
    for j in range(1, layers):
        greet((layer + j) % layers * SUBS + u, t)
    for j in range(SUBS):
        p = t * SUBS + j
        sec, core = last * SUBS + p // tps, p % tps

        @pl.when((sec != section) | (core != t))
        def _():
            greet(sec, core)

    spread_to = jnp.where(layer == last, sections - jnp.where(out_tp == t, 1, 0), 0)
    pl.semaphore_wait(barrier, (tps - 1) + (SUBS - 1) + (layers - 1) + spread_to)

    qacc[...] = jnp.zeros_like(qacc)
    kvacc[...] = jnp.zeros_like(kvacc)
    sumsq[...] = jnp.zeros_like(sumsq)
    totf[...] = jnp.zeros_like(totf)

    @pl.when(layer == 0)
    def _():
        def send(k):
            j, ci = k // chunks, k % chunks
            for e in range(1, tps):
                first_copy(j, ci, e).start()
            hbuf[t * SUBS + j, ci] = hin[j, ci]
        loop(SUBS * chunks, send)

        def arrive(k):
            j, ci = k // chunks, k % chunks
            for e in range(1, tps):
                wait_block(tp_at(e) * SUBS + j, ci)
        loop(SUBS * chunks, arrive)

    @pl.when(layer > 0)
    def _():
        def spread(ci):
            wait_block(own, ci)
            for r in range(1, SUBS):
                ag_copy(r, ci).start()
            for e in range(1, tps):
                fwd_copy(0, ci, e).start()
        loop(chunks, spread)

    def absorb(p, ci):
        x = hbuf[p, ci].astype(F32)
        sq = x * x
        part = sq[:, :HEAD_DIM]
        for i in range(1, BLOCK // HEAD_DIM):
            part = part + sq[:, i * HEAD_DIM:(i + 1) * HEAD_DIM]
        sumsq[...] += part
        scaled = (x * gain[p * chunks + ci]).astype(BF16)
        rows = pl.ds(pl.multiple_of((p * chunks + ci) * BLOCK, BLOCK), BLOCK)
        qacc[...] += dot(scaled, wq[rows, :])
        return scaled

    def near(k):
        ci, e = k // tps, k % tps
        d = tp_at(e)

        @pl.when((layer > 0) & (e > 0))
        def _():
            wait_block(u * tps + d, ci)
        scaled = absorb(u * tps + d, ci)
        rows = pl.ds(pl.multiple_of((d * chunks + ci) * BLOCK, BLOCK), BLOCK)
        kvacc[...] += dot(scaled, jnp.concatenate([wk[rows, :], wv[rows, :]], axis=1))
    loop(chunks * tps, near)

    kvst[...] = kvacc[...].astype(BF16)
    for r in range(1, SUBS):
        kvp_copy(r).start()

    def across(k):
        ci, r = k // (SUBS - 1), k % (SUBS - 1) + 1
        p = sub_at(r) * tps + t

        @pl.when(layer > 0)
        def _():
            wait_block(p, ci)
            for e in range(1, tps):
                fwd_copy(r, ci, e).start()
        absorb(p, ci)
    loop(chunks * (SUBS - 1), across)

    def far(k):
        ci, r = k // (SUBS - 1), k % (SUBS - 1) + 1
        for e in range(1, tps):
            p = sub_at(r) * tps + tp_at(e)

            @pl.when(layer > 0)
            def _():
                wait_block(p, ci)
            absorb(p, ci)
    loop(chunks * (SUBS - 1), far)

    scale = lax.rsqrt(jnp.sum(sumsq[...], axis=1, keepdims=True) / depth + NORM_EPS)
    kv = kvacc[...]
    for r in range(1, SUBS):
        kvp_copy(r).wait_recv()
        kv = kv + kvrecv[r - 1].astype(F32)
    kv = kv * scale

    def rotate(x):
        return x * cosf[...] + pltpu.roll(x, HEAD_DIM // 2, 1) * sinf[...]

    kvb[:, :HEAD_DIM] = rotate(kv[:, :HEAD_DIM]).astype(BF16)
    kvb[:, HEAD_DIM:] = kv[:, HEAD_DIM:].astype(BF16)
    for g in range(att.shape[1] // HEAD_DIM):
        cols = slice(g * HEAD_DIM, (g + 1) * HEAD_DIM)
        query = rotate(qacc[:, cols] * scale).astype(BF16)
        scores = lax.dot_general(
            query, kvb[:, :HEAD_DIM], (((1,), (1,)), ((), ())), preferred_element_type=F32
        ) * (1.0 / math.sqrt(HEAD_DIM))
        weights = jnp.where(mask[...] > 0.0, jnp.exp(scores), 0.0)
        probs = (weights / jnp.sum(weights, axis=1, keepdims=True)).astype(BF16)
        att[:, cols] = dot(probs, kvb[:, HEAD_DIM:]).astype(BF16)

    def term(p, ci):
        cols = pl.ds(pl.multiple_of((p * chunks + ci) * BLOCK, BLOCK), BLOCK)
        return dot(att[...], wo[:, cols]).astype(BF16)

    steps = chunks * SUBS

    def project(k):
        @pl.when(k < steps)
        def _():
            ci, r = k // SUBS, (k + 1) % SUBS
            v = sub_at(r)
            for e in range(1, tps):
                s1out[r, ci, e - 1] = term(v * tps + tp_at(e), ci)
                s1_copy(r, ci, e).start()
            s1own[r, ci] = term(v * tps + t, ci)

        @pl.when(k >= LAG)
        def _():
            ci, r = (k - LAG) // SUBS, (k - LAG + 1) % SUBS
            total = s1own[r, ci].astype(F32)
            for e in range(1, tps):
                s1_copy(r, ci, e).wait_recv()
                total = total + s1in[r, ci, e - 1].astype(F32)
            s1own[r, ci] = total.astype(BF16)

            @pl.when(r > 0)
            def _():
                s2_copy(r, ci).start()
    loop(steps + LAG, project)

    def deliver(j):
        pickst[j] = dot(pick[j], kvb[...]).astype(BF16)

        @pl.when(j == layer)
        def _():
            kvbuf[layer] = pickst[j]

        @pl.when(j != layer)
        def _():
            pick_copy(j).start()
    loop(layers, deliver)

    def finish(ci):
        total = hbuf[own, ci].astype(F32)
        terms = s1own[0, ci].astype(F32)
        for r in range(1, SUBS):
            s2_copy(r, ci).wait_recv()
            terms = terms + s2in[r - 1, ci].astype(F32)
        total = total + terms

        @pl.when(layer < last)
        def _():
            upd[ci] = total.astype(BF16)
            z_copy(ci).start()

        @pl.when(layer == last)
        def _():
            totf[:tokens] = total
            for s in range(sections):
                fst[s, ci] = totf[s * own_tokens:s * own_tokens + fst.shape[2]].astype(BF16)
    loop(chunks, finish)

    @pl.when(layer == last)
    def _():
        def out(s):
            mine = (s == section) & (out_tp == t)

            @pl.when(mine)
            def _():
                fin[out_slot] = fst[s]

            @pl.when(jnp.logical_not(mine))
            def _():
                fin_copy(s).start()
        loop(sections, out)

    def kv_in(j):
        @pl.when(j != layer)
        def _():
            copy(pickst.at[j], kvbuf.at[j], pk_s.at[j], pk_r.at[j], j * SUBS + u, t).wait_recv()
    loop(layers, kv_in)
    kv_out[...] = kvbuf[...]

    def fin_in(j):
        p = t * SUBS + j
        sec, core = last * SUBS + p // tps, p % tps

        @pl.when((sec != section) | (core != t))
        def _():
            copy(fst.at[0], fin.at[j], fin_s.at[0], fin_r.at[j], sec, core).wait_recv()
    loop(SUBS, fin_in)
    fin_out[...] = fin[...]

    @pl.when(layer == 0)
    def _():
        def sent(k):
            for e in range(1, tps):
                first_copy(k // chunks, k % chunks, e).wait_send()
        loop(SUBS * chunks, sent)

    @pl.when(layer > 0)
    def _():
        def sent(ci):
            for r in range(SUBS):
                for e in range(1, tps):
                    fwd_copy(r, ci, e).wait_send()
            for r in range(1, SUBS):
                ag_copy(r, ci).wait_send()
        loop(chunks, sent)

    for r in range(1, SUBS):
        kvp_copy(r).wait_send()

    def sums_sent(ci):
        for r in range(SUBS):
            for e in range(1, tps):
                s1_copy(r, ci, e).wait_send()
        for r in range(1, SUBS):
            s2_copy(r, ci).wait_send()

        @pl.when(layer < last)
        def _():
            z_copy(ci).wait_send()
    loop(chunks, sums_sent)

    def kv_sent(j):
        @pl.when(j != layer)
        def _():
            pick_copy(j).wait_send()
    loop(layers, kv_sent)

    @pl.when(layer == last)
    def _():
        def sent(s):
            @pl.when(jnp.logical_not((s == section) & (out_tp == t)))
            def _():
                fin_copy(s).wait_send()
        loop(sections, sent)


def shards(
    hidden_t, norm_gain, q_weight, k_weight, v_weight, o_weight, lengths, prior_offsets, owners
):
    sections = lax.axis_size("section")
    tps = lax.axis_size("tp")
    section = lax.axis_index("section")
    layers = sections // SUBS
    layer = section // SUBS
    sub = section % SUBS
    rows_dev, tokens = hidden_t.shape
    num_reqs = lengths.shape[0]
    capacity = 2 * tokens // num_reqs
    cap_pad = round_up(capacity, 16)
    own_tokens = tokens // sections
    tok_pad = round_up(own_tokens, 16)
    pieces = SUBS * tps
    chunks = rows_dev // SUBS // BLOCK
    q_cols = q_weight.shape[2]

    req_ends = jnp.cumsum(lengths)
    req_starts = req_ends - lengths
    tok_ids = jnp.arange(tokens, dtype=jnp.int32)
    req_ids = jnp.arange(num_reqs, dtype=jnp.int32)
    req_of_tok = jnp.sum((tok_ids[:, None] >= req_ends[None, :]).astype(jnp.int32), axis=1)
    req_onehot = req_of_tok[:, None] == req_ids[None, :]
    positions = (
        jnp.sum(jnp.where(req_onehot, (prior_offsets - req_starts)[None, :], 0), axis=1) + tok_ids
    )
    mask = (
        (req_of_tok[:, None] == req_of_tok[None, :]) & (tok_ids[None, :] <= tok_ids[:, None])
    ).astype(F32)
    half = HEAD_DIM // 2
    inv_freq = jnp.power(F32(ROPE_BASE), -(2.0 * jnp.arange(half, dtype=F32)) / HEAD_DIM)
    angle = positions.astype(F32)[:, None] * inv_freq[None, :]
    cos, sin = jnp.cos(angle), jnp.sin(angle)
    cosf = jnp.concatenate([cos, cos], axis=1)
    sinf = jnp.concatenate([-sin, sin], axis=1)

    mine = jnp.arange(layers, dtype=jnp.int32) * SUBS + sub
    chosen = owners[None, :] == mine[:, None]
    start = jnp.sum(jnp.where(chosen, req_starts[None, :], 0), axis=1)
    count = jnp.sum(jnp.where(chosen, lengths[None, :], 0), axis=1)
    slots = jnp.arange(cap_pad, dtype=jnp.int32)
    pick = (
        (tok_ids[None, None, :] == start[:, None, None] + slots[None, :, None])
        & (slots[None, :, None] < count[:, None, None])
    ).astype(BF16)

    gain = lax.dynamic_index_in_dim(norm_gain, layer, 0, keepdims=False).astype(F32)
    gain = gain.reshape(pieces * chunks, 1, BLOCK)
    hin = hidden_t.reshape(SUBS, chunks, BLOCK, tokens).transpose(0, 1, 3, 2)

    vm = pltpu.VMEM
    dma = pltpu.SemaphoreType.DMA
    others = tps - 1
    far_subs = SUBS - 1
    blk = (tokens, BLOCK)
    fin, kv = pl.pallas_call(
        functools.partial(relay_kernel, layers, tps, own_tokens),
        out_shape=(
            jax.ShapeDtypeStruct((SUBS, chunks, tok_pad, BLOCK), BF16),
            jax.ShapeDtypeStruct((layers, cap_pad, 2 * HEAD_DIM), BF16),
        ),
        in_specs=[pl.BlockSpec(memory_space=pltpu.VMEM)] * 10,
        out_specs=(pl.BlockSpec(memory_space=pltpu.VMEM),) * 2,
        scratch_shapes=[
            vm((pieces, chunks) + blk, BF16),
            vm((tokens, q_cols), F32),
            vm((tokens, 2 * HEAD_DIM), F32),
            vm((tokens, HEAD_DIM), F32),
            vm((tokens, 2 * HEAD_DIM), BF16),
            vm((far_subs, tokens, 2 * HEAD_DIM), BF16),
            vm((tokens, 2 * HEAD_DIM), BF16),
            vm((tokens, q_cols), BF16),
            vm((SUBS, chunks, others) + blk, BF16),
            vm((SUBS, chunks, others) + blk, BF16),
            vm((SUBS, chunks) + blk, BF16),
            vm((far_subs, chunks) + blk, BF16),
            vm((chunks,) + blk, BF16),
            vm((tokens + 32, BLOCK), F32),
            vm((sections, chunks, tok_pad, BLOCK), BF16),
            vm((SUBS, chunks, tok_pad, BLOCK), BF16),
            vm((layers, cap_pad, 2 * HEAD_DIM), BF16),
            vm((layers, cap_pad, 2 * HEAD_DIM), BF16),
            dma((pieces, chunks)),
            dma((SUBS, chunks, others)),
            dma((far_subs, chunks)),
            dma((far_subs,)),
            dma((far_subs,)),
            dma((SUBS, chunks, others)),
            dma((SUBS, chunks, others)),
            dma((far_subs, chunks)),
            dma((far_subs, chunks)),
            dma((chunks,)),
            dma((layers,)),
            dma((layers,)),
            dma((sections,)),
            dma((SUBS,)),
        ],
        compiler_params=pltpu.CompilerParams(
            collective_id=0, has_side_effects=True, vmem_limit_bytes=56 * 1024 * 1024
        ),
        name="relay",
    )(hin, gain, q_weight[0], k_weight[0], v_weight[0], o_weight[0], cosf, sinf, mask, pick)
    final_hidden = fin[:, :, :own_tokens].transpose(0, 1, 3, 2).reshape(rows_dev, own_tokens)
    return final_hidden, kv[None, :, :capacity]


def solution(mesh):
    return jax.shard_map(
        shards,
        mesh=mesh,
        in_specs=(
            P("tp", None),
            P(),
            P("section", None, "tp"),
            P("section", None, "tp"),
            P("section", None, "tp"),
            P("section", "tp", None),
            P(),
            P(),
            P(),
        ),
        out_specs=(P("tp", "section"), P("section", None, None, "tp")),
        check_vma=False,
    )
```

```python
import functools
import math

import jax
import jax.numpy as jnp
from jax import lax
from jax.experimental import pallas as pl
from jax.experimental.pallas import tpu as pltpu
from jax.sharding import PartitionSpec as P

HEAD_DIM = 128
SUBS = 4
BLOCK = 256
GROUP = 2
SPLIT = 4
NORM_EPS = 1e-05
ROPE_BASE = 500000.0
MESH = pl.DeviceIdType.MESH
F32 = jnp.float32
BF16 = jnp.bfloat16


def dot(a, b):
    return jnp.dot(a, b, preferred_element_type=F32)


def round_up(count, unit):
    return (count + unit - 1) // unit * unit


def relay_kernel(
    layers, tps, own_tokens,
    hin, gain, wq, wk, wv, wo, cosf, sinf, mask, pick,
    fin_out, kv_out,
    hbuf, qacc, kvacc, sumsq, kvst, kvrecv, kvb, att,
    s1out, s1in, s1own, s2in, upd, totf, fst, fin, pickst, kvbuf,
    hs, fwd_s, ag_s, kvp_s, kvp_r, s1_s, s1_r, s2_s, s2_r, z_s, pk_s, pk_r, fin_s, fin_r,
):
    section = lax.axis_index("section")
    t = lax.axis_index("tp")
    layer = section // SUBS
    u = section % SUBS
    splits, pieces, chunks, span, block = hbuf.shape
    depth = pieces * chunks * block
    group = min(GROUP, chunks)
    per_split = layers * SUBS // splits
    own = u * tps + t
    sections = layers * SUBS
    last = layers - 1
    out_tp = own // SUBS
    out_slot = own % SUBS
    base = layer * SUBS

    def copy(src, dst, send, recv, sec, core):
        return pltpu.make_async_remote_copy(
            src_ref=src, dst_ref=dst, send_sem=send, recv_sem=recv,
            device_id=(sec, core), device_id_type=MESH,
        )

    def sub_at(r):
        return (u + r) % SUBS

    def tp_at(e):
        return (t + e) % tps

    def first_copy(i, j, ci, e):
        p = t * SUBS + j
        return copy(hbuf.at[i, p, ci], hbuf.at[i, p, ci], fwd_s.at[i, j, ci, e - 1], hs.at[i, p, ci],
                    section, tp_at(e))

    def fwd_copy(i, r, ci, e):
        p = sub_at(r) * tps + t
        return copy(hbuf.at[i, p, ci], hbuf.at[i, p, ci], fwd_s.at[i, r, ci, e - 1], hs.at[i, p, ci],
                    section, tp_at(e))

    def ag_copy(i, r, ci):
        return copy(hbuf.at[i, own, ci], hbuf.at[i, own, ci], ag_s.at[i, r - 1, ci], hs.at[i, own, ci],
                    base + sub_at(r), t)

    def wait_block(i, p, ci):
        copy(hbuf.at[i, p, ci], hbuf.at[i, p, ci], fwd_s.at[0, 0, 0, 0], hs.at[i, p, ci],
             section, tp_at(1)).wait_recv()

    def kvp_copy(i, r):
        return copy(kvst.at[i], kvrecv.at[i, r - 1], kvp_s.at[i, r - 1], kvp_r.at[i, r - 1],
                    base + sub_at(r), t)

    def s1_copy(i, r, ci, e):
        return copy(s1out.at[i, r, ci, e - 1], s1in.at[i, r, ci, e - 1], s1_s.at[i, r, ci, e - 1],
                    s1_r.at[i, r, ci, e - 1], section, tp_at(e))

    def s2_copy(i, r, ci):
        return copy(s1own.at[i, r, ci], s2in.at[i, r - 1, ci], s2_s.at[i, r - 1, ci], s2_r.at[i, r - 1, ci],
                    base + sub_at(r), t)

    def z_copy(i, ci):
        return copy(upd.at[i, ci], hbuf.at[i, own, ci], z_s.at[i, ci], hs.at[i, own, ci], section + SUBS, t)

    def pick_copy(j):
        return copy(pickst.at[j], kvbuf.at[layer], pk_s.at[j], pk_r.at[layer], j * SUBS + u, t)

    def fin_copy(s):
        return copy(fst.at[s], fin.at[out_slot], fin_s.at[s], fin_r.at[out_slot], s, out_tp)

    def loop(count, body):
        def step(k, carry):
            body(k)
            return carry
        lax.fori_loop(0, count, step, jnp.int32(0))

    barrier = pltpu.get_barrier_semaphore()

    def greet(sec, core):
        pl.semaphore_signal(barrier, inc=1, device_id=(sec, core), device_id_type=MESH)

    for e in range(1, tps):
        greet(section, tp_at(e))
    for r in range(1, SUBS):
        greet(base + sub_at(r), t)
    for j in range(1, layers):
        greet((layer + j) % layers * SUBS + u, t)
    for j in range(SUBS):
        p = t * SUBS + j
        sec, core = last * SUBS + p // tps, p % tps

        @pl.when((sec != section) | (core != t))
        def _():
            greet(sec, core)

    spread_to = jnp.where(layer == last, sections - jnp.where(out_tp == t, 1, 0), 0)
    pl.semaphore_wait(barrier, (tps - 1) + (SUBS - 1) + (layers - 1) + spread_to)

    totf[...] = jnp.zeros_like(totf)
    kvb[0] = jnp.zeros_like(kvb[0])

    @pl.when(layer == 0)
    def _():
        def send(k):
            j, ci = k // chunks, k % chunks
            rows = pl.ds(pl.multiple_of(k * block, block), block)
            turned = hin[rows, :].astype(F32).T.astype(BF16)
            for i in range(splits):
                hbuf[i, t * SUBS + j, ci] = turned[i * span:(i + 1) * span]
                for e in range(1, tps):
                    first_copy(i, j, ci, e).start()
        loop(SUBS * chunks, send)

    def spread(i, ci):
        wait_block(i, own, ci)
        for r in range(1, SUBS):
            ag_copy(i, r, ci).start()
        for e in range(1, tps):
            fwd_copy(i, 0, ci, e).start()

    def rotate(x, i):
        return x * cosf[i] + pltpu.roll(x, HEAD_DIM // 2, 1) * sinf[i]

    def stage(i):
        qacc[...] = jnp.zeros_like(qacc)
        kvacc[...] = jnp.zeros_like(kvacc)
        sumsq[...] = jnp.zeros_like(sumsq)

        @pl.when(layer == 0)
        def _():
            def arrive(k):
                j, ci = k // chunks, k % chunks
                for e in range(1, tps):
                    wait_block(i, tp_at(e) * SUBS + j, ci)
            loop(SUBS * chunks, arrive)

        @pl.when((layer > 0) & (i == 0))
        def _():
            loop(chunks, lambda ci: spread(0, ci))

        def absorb(p, n):
            parts, squares = [], 0.0
            for m in range(group):
                ci = n * group + m
                x = hbuf[i, p, ci].astype(F32)
                sq = x * x
                for w in range(block // HEAD_DIM):
                    squares = squares + sq[:, w * HEAD_DIM:(w + 1) * HEAD_DIM]
                parts.append((x * gain[p * chunks + ci]).astype(BF16))
            scaled = jnp.concatenate(parts, axis=1)
            width = group * block
            rows = pl.ds(pl.multiple_of(p * chunks * block + n * width, width), width)
            return scaled, dot(scaled, wq[rows, :]), squares

        def near(n):
            for m in range(group):
                for e in range(1, tps):
                    @pl.when(layer > 0)
                    def _():
                        wait_block(i, u * tps + tp_at(e), n * group + m)
            query_sum, square_sum, kv_sum = 0.0, 0.0, 0.0
            width = group * block
            for e in range(tps):
                d = tp_at(e)
                scaled, query, squares = absorb(u * tps + d, n)
                query_sum, square_sum = query_sum + query, square_sum + squares
                rows = pl.ds(pl.multiple_of(d * chunks * block + n * width, width), width)
                kv_sum = kv_sum + dot(scaled, jnp.concatenate([wk[rows, :], wv[rows, :]], axis=1))
            qacc[...] += query_sum
            sumsq[...] += square_sum
            kvacc[...] += kv_sum
        loop(chunks // group, near)

        kvst[i] = kvacc[...].astype(BF16)
        for r in range(1, SUBS):
            kvp_copy(i, r).start()

        def take(n, core):
            query_sum, square_sum = 0.0, 0.0
            for r in range(1, SUBS):
                scaled, query, squares = absorb(sub_at(r) * tps + core, n)
                query_sum, square_sum = query_sum + query, square_sum + squares
            qacc[...] += query_sum
            sumsq[...] += square_sum

        def across(n):
            @pl.when(layer > 0)
            def _():
                for m in range(group):
                    for r in range(1, SUBS):
                        ci = n * group + m
                        wait_block(i, sub_at(r) * tps + t, ci)
                        for e in range(1, tps):
                            fwd_copy(i, r, ci, e).start()
            take(n, t)
        loop(chunks // group, across)

        def far(n):
            for e in range(1, tps):
                @pl.when(layer > 0)
                def _():
                    for m in range(group):
                        for r in range(1, SUBS):
                            wait_block(i, sub_at(r) * tps + tp_at(e), n * group + m)
                take(n, tp_at(e))
        loop(chunks // group, far)

        scale = lax.rsqrt(jnp.sum(sumsq[...], axis=1, keepdims=True) / depth + NORM_EPS)
        kv = kvacc[...]
        for r in range(1, SUBS):
            kvp_copy(i, r).wait_recv()
            kv = kv + kvrecv[i, r - 1].astype(F32)
        kv = kv * scale
        kvb[i + 1, :, :HEAD_DIM] = rotate(kv[:, :HEAD_DIM], i).astype(BF16)
        kvb[i + 1, :, HEAD_DIM:] = kv[:, HEAD_DIM:].astype(BF16)
        both = jnp.concatenate([kvb[i], kvb[i + 1]], axis=0)
        for g in range(att.shape[1] // HEAD_DIM):
            cols = slice(g * HEAD_DIM, (g + 1) * HEAD_DIM)
            query = rotate(qacc[:, cols] * scale, i).astype(BF16)
            scores = lax.dot_general(
                query, both[:, :HEAD_DIM], (((1,), (1,)), ((), ())), preferred_element_type=F32
            ) * (1.0 / math.sqrt(HEAD_DIM))
            weights = jnp.where(mask[i] > 0.0, jnp.exp(scores), 0.0)
            probs = (weights / jnp.sum(weights, axis=1, keepdims=True)).astype(BF16)
            att[:, cols] = dot(probs, both[:, HEAD_DIM:]).astype(BF16)

        def term(p, ci):
            cols = pl.ds(pl.multiple_of((p * chunks + ci) * block, block), block)
            return dot(att[...], wo[:, cols]).astype(BF16)

        def project(k):
            @pl.when(k < chunks)
            def _():
                for e in range(1, tps):
                    for r in (1, 2, 3, 0):
                        s1out[i, r, k, e - 1] = term(sub_at(r) * tps + tp_at(e), k)
                    for r in (1, 2, 3, 0):
                        s1_copy(i, r, k, e).start()
                for r in range(SUBS):
                    s1own[i, r, k] = term(sub_at(r) * tps + t, k)

            @pl.when(k >= 1)
            def _():
                ci = k - 1
                for r in (1, 2, 3, 0):
                    total = s1own[i, r, ci].astype(F32)
                    for e in range(1, tps):
                        s1_copy(i, r, ci, e).wait_recv()
                        total = total + s1in[i, r, ci, e - 1].astype(F32)
                    s1own[i, r, ci] = total.astype(BF16)
                    if r > 0:
                        s2_copy(i, r, ci).start()
        loop(chunks + 1, project)

        @pl.when(i == splits - 1)
        def _():
            def deliver(j):
                rows = dot(pick[j, 0], kvb[1])
                for n in range(1, splits):
                    rows = rows + dot(pick[j, n], kvb[n + 1])
                pickst[j] = rows.astype(BF16)

                @pl.when(j == layer)
                def _():
                    kvbuf[layer] = pickst[j]

                @pl.when(j != layer)
                def _():
                    pick_copy(j).start()
            loop(layers, deliver)

        def finish(ci):
            @pl.when(ci < chunks)
            def _():
                terms = s1own[i, 0, ci].astype(F32)
                for r in range(1, SUBS):
                    s2_copy(i, r, ci).wait_recv()
                    terms = terms + s2in[i, r - 1, ci].astype(F32)
                total = hbuf[i, own, ci].astype(F32) + terms

                @pl.when(layer < last)
                def _():
                    upd[i, ci] = total.astype(BF16)
                    z_copy(i, ci).start()

                @pl.when(layer == last)
                def _():
                    totf[:span] = total
                    for n in range(per_split):
                        rows = totf[n * own_tokens:n * own_tokens + fst.shape[2]]
                        fst[i * per_split + n, ci] = rows.astype(BF16)

            @pl.when((ci >= 1) & (layer > 0) & (i < splits - 1))
            def _():
                spread(i + 1, ci - 1)
        loop(chunks + 1, finish)

        @pl.when(layer == last)
        def _():
            def out(n):
                s = i * per_split + n
                mine = (s == section) & (out_tp == t)

                @pl.when(mine)
                def _():
                    fin[out_slot] = fst[s]

                @pl.when(jnp.logical_not(mine))
                def _():
                    fin_copy(s).start()
            loop(per_split, out)

    loop(splits, stage)

    def kv_in(j):
        @pl.when(j != layer)
        def _():
            copy(pickst.at[j], kvbuf.at[j], pk_s.at[j], pk_r.at[j], j * SUBS + u, t).wait_recv()
    loop(layers, kv_in)
    kv_out[...] = kvbuf[...]

    def fin_in(j):
        p = t * SUBS + j
        sec, core = last * SUBS + p // tps, p % tps

        @pl.when((sec != section) | (core != t))
        def _():
            copy(fst.at[0], fin.at[j], fin_s.at[0], fin_r.at[j], sec, core).wait_recv()
    loop(SUBS, fin_in)
    fin_out[...] = fin[...]

    @pl.when(layer == 0)
    def _():
        def sent(k):
            for e in range(1, tps):
                first_copy(k // (SUBS * chunks), k // chunks % SUBS, k % chunks, e).wait_send()
        loop(splits * SUBS * chunks, sent)

    @pl.when(layer > 0)
    def _():
        def sent(k):
            i, ci = k // chunks, k % chunks
            for r in range(SUBS):
                for e in range(1, tps):
                    fwd_copy(i, r, ci, e).wait_send()
            for r in range(1, SUBS):
                ag_copy(i, r, ci).wait_send()
        loop(splits * chunks, sent)

    def kvp_sent(i):
        for r in range(1, SUBS):
            kvp_copy(i, r).wait_send()
    loop(splits, kvp_sent)

    def sums_sent(k):
        i, ci = k // chunks, k % chunks
        for r in range(SUBS):
            for e in range(1, tps):
                s1_copy(i, r, ci, e).wait_send()
        for r in range(1, SUBS):
            s2_copy(i, r, ci).wait_send()

        @pl.when(layer < last)
        def _():
            z_copy(i, ci).wait_send()
    loop(splits * chunks, sums_sent)

    def kv_sent(j):
        @pl.when(j != layer)
        def _():
            pick_copy(j).wait_send()
    loop(layers, kv_sent)

    @pl.when(layer == last)
    def _():
        def sent(s):
            @pl.when(jnp.logical_not((s == section) & (out_tp == t)))
            def _():
                fin_copy(s).wait_send()
        loop(sections, sent)


def shards(
    hidden_t, norm_gain, q_weight, k_weight, v_weight, o_weight, lengths, prior_offsets, owners
):
    sections = lax.axis_size("section")
    tps = lax.axis_size("tp")
    section = lax.axis_index("section")
    layers = sections // SUBS
    layer = section // SUBS
    sub = section % SUBS
    rows_dev, tokens = hidden_t.shape
    num_reqs = lengths.shape[0]
    capacity = 2 * tokens // num_reqs
    cap_pad = round_up(capacity, 16)
    own_tokens = tokens // sections
    tok_pad = round_up(own_tokens, 16)
    pieces = SUBS * tps
    block = min(BLOCK, rows_dev // SUBS)
    chunks = rows_dev // SUBS // block
    q_cols = q_weight.shape[2]
    span = tokens // SPLIT
    assert span >= capacity and sections % SPLIT == 0 and span % 16 == 0

    req_ends = jnp.cumsum(lengths)
    req_starts = req_ends - lengths
    tok_ids = jnp.arange(tokens, dtype=jnp.int32)
    req_ids = jnp.arange(num_reqs, dtype=jnp.int32)
    req_of_tok = jnp.sum((tok_ids[:, None] >= req_ends[None, :]).astype(jnp.int32), axis=1)
    req_onehot = req_of_tok[:, None] == req_ids[None, :]
    positions = (
        jnp.sum(jnp.where(req_onehot, (prior_offsets - req_starts)[None, :], 0), axis=1) + tok_ids
    )
    spans = jnp.arange(SPLIT, dtype=jnp.int32)[:, None, None] * span
    query_ids = spans + jnp.arange(span, dtype=jnp.int32)[None, :, None]
    key_ids = spans + jnp.arange(-span, span, dtype=jnp.int32)[None, None, :]
    first_ids = jnp.sum(jnp.where(req_onehot, req_starts[None, :], 0), axis=1).reshape(SPLIT, span, 1)
    mask = ((key_ids >= first_ids) & (key_ids <= query_ids)).astype(F32)
    half = HEAD_DIM // 2
    inv_freq = jnp.power(F32(ROPE_BASE), -(2.0 * jnp.arange(half, dtype=F32)) / HEAD_DIM)
    angle = positions.astype(F32)[:, None] * inv_freq[None, :]
    cos, sin = jnp.cos(angle), jnp.sin(angle)
    cosf = jnp.concatenate([cos, cos], axis=1).reshape(SPLIT, span, HEAD_DIM)
    sinf = jnp.concatenate([-sin, sin], axis=1).reshape(SPLIT, span, HEAD_DIM)

    mine = jnp.arange(layers, dtype=jnp.int32) * SUBS + sub
    chosen = owners[None, :] == mine[:, None]
    start = jnp.sum(jnp.where(chosen, req_starts[None, :], 0), axis=1)
    count = jnp.sum(jnp.where(chosen, lengths[None, :], 0), axis=1)
    slots = jnp.arange(cap_pad, dtype=jnp.int32)
    tok_split = tok_ids.reshape(1, SPLIT, 1, span)
    slots = slots[None, None, :, None]
    pick = (
        (tok_split == start[:, None, None, None] + slots) & (slots < count[:, None, None, None])
    ).astype(BF16)

    gain = lax.dynamic_index_in_dim(norm_gain, layer, 0, keepdims=False).astype(F32)
    gain = gain.reshape(pieces * chunks, 1, block)

    vm = pltpu.VMEM
    dma = pltpu.SemaphoreType.DMA
    others = tps - 1
    far_subs = SUBS - 1
    blk = (span, block)
    kv_cols = 2 * HEAD_DIM
    fin, kv = pl.pallas_call(
        functools.partial(relay_kernel, layers, tps, own_tokens),
        out_shape=(
            jax.ShapeDtypeStruct((SUBS, chunks, tok_pad, block), BF16),
            jax.ShapeDtypeStruct((layers, cap_pad, 2 * HEAD_DIM), BF16),
        ),
        in_specs=[pl.BlockSpec(memory_space=pltpu.VMEM)] * 10,
        out_specs=(pl.BlockSpec(memory_space=pltpu.VMEM),) * 2,
        scratch_shapes=[
            vm((SPLIT, pieces, chunks) + blk, BF16),
            vm((span, q_cols), F32),
            vm((span, kv_cols), F32),
            vm((span, HEAD_DIM), F32),
            vm((SPLIT, span, kv_cols), BF16),
            vm((SPLIT, far_subs, span, kv_cols), BF16),
            vm((SPLIT + 1, span, kv_cols), BF16),
            vm((span, q_cols), BF16),
            vm((SPLIT, SUBS, chunks, others) + blk, BF16),
            vm((SPLIT, SUBS, chunks, others) + blk, BF16),
            vm((SPLIT, SUBS, chunks) + blk, BF16),
            vm((SPLIT, far_subs, chunks) + blk, BF16),
            vm((SPLIT, chunks) + blk, BF16),
            vm((span + 32, block), F32),
            vm((sections, chunks, tok_pad, block), BF16),
            vm((SUBS, chunks, tok_pad, block), BF16),
            vm((layers, cap_pad, 2 * HEAD_DIM), BF16),
            vm((layers, cap_pad, 2 * HEAD_DIM), BF16),
            dma((SPLIT, pieces, chunks)),
            dma((SPLIT, SUBS, chunks, others)),
            dma((SPLIT, far_subs, chunks)),
            dma((SPLIT, far_subs)),
            dma((SPLIT, far_subs)),
            dma((SPLIT, SUBS, chunks, others)),
            dma((SPLIT, SUBS, chunks, others)),
            dma((SPLIT, far_subs, chunks)),
            dma((SPLIT, far_subs, chunks)),
            dma((SPLIT, chunks)),
            dma((layers,)),
            dma((layers,)),
            dma((sections,)),
            dma((SUBS,)),
        ],
        compiler_params=pltpu.CompilerParams(
            collective_id=0, has_side_effects=True, vmem_limit_bytes=56 * 1024 * 1024
        ),
        name="relay",
    )(hidden_t, gain, q_weight[0], k_weight[0], v_weight[0], o_weight[0], cosf, sinf, mask, pick)
    final_hidden = fin[:, :, :own_tokens].transpose(0, 1, 3, 2).reshape(rows_dev, own_tokens)
    return final_hidden, kv[None, :, :capacity]


def solution(mesh):
    return jax.shard_map(
        shards,
        mesh=mesh,
        in_specs=(
            P("tp", None),
            P(),
            P("section", None, "tp"),
            P("section", None, "tp"),
            P("section", None, "tp"),
            P("section", "tp", None),
            P(),
            P(),
            P(),
        ),
        out_specs=(P("tp", "section"), P("section", None, None, "tp")),
        check_vma=False,
    )
```

```python
import functools
import math

import jax
import jax.numpy as jnp
from jax import lax
from jax.experimental import pallas as pl
from jax.experimental.pallas import tpu as pltpu
from jax.sharding import PartitionSpec as P

HEAD_DIM = 128
SUBS = 4
BLOCK = 256
GROUP = 2
SPLIT = 4
NORM_EPS = 1e-05
ROPE_BASE = 500000.0
MESH = pl.DeviceIdType.MESH
F32 = jnp.float32
BF16 = jnp.bfloat16


def dot(a, b):
    return jnp.dot(a, b, preferred_element_type=F32)


def round_up(count, unit):
    return (count + unit - 1) // unit * unit


def relay_kernel(
    layers, tps, own_tokens,
    hin, gain, wq, wk, wv, wo, cosf, sinf, mask, pick,
    fin_out, kv_out,
    hbuf, qacc, kvacc, sumsq, kvst, kvrecv, kvb, att,
    s1out, s1in, s1own, s2in, upd, totf, fst, fin, pickst, kvbuf,
    hs, fwd_s, ag_s, kvp_s, kvp_r, s1_s, s1_r, s2_s, s2_r, z_s, pk_s, pk_r, fin_s, fin_r,
):
    section = lax.axis_index("section")
    t = lax.axis_index("tp")
    layer = section // SUBS
    u = section % SUBS
    splits, pieces, chunks, span, block = hbuf.shape
    depth = pieces * chunks * block
    group = min(GROUP, chunks)
    per_split = layers * SUBS // splits
    own = u * tps + t
    sections = layers * SUBS
    last = layers - 1
    out_tp = own // SUBS
    out_slot = own % SUBS
    base = layer * SUBS

    def copy(src, dst, send, recv, sec, core):
        return pltpu.make_async_remote_copy(
            src_ref=src, dst_ref=dst, send_sem=send, recv_sem=recv,
            device_id=(sec, core), device_id_type=MESH,
        )

    along_x = u + 1 - 2 * (u % 2)
    along_y = (u + 2) % SUBS
    subs = (u, along_x, along_y, (along_x + 2) % SUBS)

    def sub_at(r):
        return subs[r]

    def side(which):
        return along_x + (along_y - along_x) * which

    def tp_at(e):
        return (t + e) % tps

    def first_copy(i, j, ci, e):
        p = t * SUBS + j
        return copy(hbuf.at[i, p, ci], hbuf.at[i, p, ci], fwd_s.at[i, j, ci, e - 1], hs.at[i, p, ci],
                    section, tp_at(e))

    def fwd_copy(i, r, ci, e):
        p = sub_at(r) * tps + t
        return copy(hbuf.at[i, p, ci], hbuf.at[i, p, ci], fwd_s.at[i, r, ci, e - 1], hs.at[i, p, ci],
                    section, tp_at(e))

    def ag_copy(i, r, ci):
        return copy(hbuf.at[i, own, ci], hbuf.at[i, own, ci], ag_s.at[i, r - 1, ci], hs.at[i, own, ci],
                    base + sub_at(r), t)

    def hop_copy(i, ci):
        p = side(ci % 2) * tps + t
        return copy(hbuf.at[i, p, ci], hbuf.at[i, p, ci], ag_s.at[i, 2, ci], hs.at[i, p, ci],
                    base + side(1 - ci % 2), t)

    def wait_block(i, p, ci):
        copy(hbuf.at[i, p, ci], hbuf.at[i, p, ci], fwd_s.at[0, 0, 0, 0], hs.at[i, p, ci],
             section, tp_at(1)).wait_recv()

    def kvp_copy(i, r):
        return copy(kvst.at[i], kvrecv.at[i, r - 1], kvp_s.at[i, r - 1], kvp_r.at[i, r - 1],
                    base + sub_at(r), t)

    def s1_copy(i, r, ci, e):
        return copy(s1out.at[i, r, ci, e - 1], s1in.at[i, r, ci, e - 1], s1_s.at[i, r, ci, e - 1],
                    s1_r.at[i, r, ci, e - 1], section, tp_at(e))

    def s2_copy(i, which, ci):
        return copy(s1own.at[i, which + 1, ci], s2in.at[i, which, ci], s2_s.at[i, which, ci],
                    s2_r.at[i, which, ci], base + side(which), t)

    def cross_copy(i, ci):
        return copy(s1own.at[i, 3, ci], s2in.at[i, 2, ci], s2_s.at[i, 2, ci], s2_r.at[i, 2, ci],
                    base + side(ci % 2), t)

    def z_copy(i, ci):
        return copy(upd.at[i, ci], hbuf.at[i, own, ci], z_s.at[i, ci], hs.at[i, own, ci], section + SUBS, t)

    def pick_copy(j):
        return copy(pickst.at[j], kvbuf.at[layer], pk_s.at[j], pk_r.at[layer], j * SUBS + u, t)

    def fin_copy(s):
        return copy(fst.at[s], fin.at[out_slot], fin_s.at[s], fin_r.at[out_slot], s, out_tp)

    def loop(count, body):
        def step(k, carry):
            body(k)
            return carry
        lax.fori_loop(0, count, step, jnp.int32(0))

    barrier = pltpu.get_barrier_semaphore()

    def greet(sec, core):
        pl.semaphore_signal(barrier, inc=1, device_id=(sec, core), device_id_type=MESH)

    for e in range(1, tps):
        greet(section, tp_at(e))
    for r in range(1, SUBS):
        greet(base + sub_at(r), t)
    for j in range(1, layers):
        greet((layer + j) % layers * SUBS + u, t)
    for j in range(SUBS):
        p = t * SUBS + j
        sec, core = last * SUBS + p // tps, p % tps

        @pl.when((sec != section) | (core != t))
        def _():
            greet(sec, core)

    spread_to = jnp.where(layer == last, sections - jnp.where(out_tp == t, 1, 0), 0)
    pl.semaphore_wait(barrier, (tps - 1) + (SUBS - 1) + (layers - 1) + spread_to)

    totf[...] = jnp.zeros_like(totf)
    kvb[0] = jnp.zeros_like(kvb[0])

    @pl.when(layer == 0)
    def _():
        def send(k):
            j, ci = k // chunks, k % chunks
            rows = pl.ds(pl.multiple_of(k * block, block), block)
            turned = hin[rows, :].astype(F32).T.astype(BF16)
            for i in range(splits):
                hbuf[i, t * SUBS + j, ci] = turned[i * span:(i + 1) * span]
                for e in range(1, tps):
                    first_copy(i, j, ci, e).start()
        loop(SUBS * chunks, send)

    def spread(i, ci):
        wait_block(i, own, ci)
        for r in (1, 2):
            ag_copy(i, r, ci).start()
        for e in range(1, tps):
            fwd_copy(i, 0, ci, e).start()

    def rotate(x, i):
        return x * cosf[i] + pltpu.roll(x, HEAD_DIM // 2, 1) * sinf[i]

    def stage(i):
        qacc[...] = jnp.zeros_like(qacc)
        kvacc[...] = jnp.zeros_like(kvacc)
        sumsq[...] = jnp.zeros_like(sumsq)

        @pl.when(layer == 0)
        def _():
            def arrive(k):
                j, ci = k // chunks, k % chunks
                for e in range(1, tps):
                    wait_block(i, tp_at(e) * SUBS + j, ci)
            loop(SUBS * chunks, arrive)

        @pl.when((layer > 0) & (i == 0))
        def _():
            loop(chunks, lambda ci: spread(0, ci))

        def absorb(p, n):
            parts, squares = [], 0.0
            for m in range(group):
                ci = n * group + m
                x = hbuf[i, p, ci].astype(F32)
                sq = x * x
                for w in range(block // HEAD_DIM):
                    squares = squares + sq[:, w * HEAD_DIM:(w + 1) * HEAD_DIM]
                parts.append((x * gain[p * chunks + ci]).astype(BF16))
            scaled = jnp.concatenate(parts, axis=1)
            width = group * block
            rows = pl.ds(pl.multiple_of(p * chunks * block + n * width, width), width)
            return scaled, dot(scaled, wq[rows, :]), squares

        def near(n):
            for m in range(group):
                for e in range(1, tps):
                    @pl.when(layer > 0)
                    def _():
                        wait_block(i, u * tps + tp_at(e), n * group + m)
            query_sum, square_sum, kv_sum = 0.0, 0.0, 0.0
            width = group * block
            for e in range(tps):
                d = tp_at(e)
                scaled, query, squares = absorb(u * tps + d, n)
                query_sum, square_sum = query_sum + query, square_sum + squares
                rows = pl.ds(pl.multiple_of(d * chunks * block + n * width, width), width)
                kv_sum = kv_sum + dot(scaled, jnp.concatenate([wk[rows, :], wv[rows, :]], axis=1))
            qacc[...] += query_sum
            sumsq[...] += square_sum
            kvacc[...] += kv_sum
        loop(chunks // group, near)

        kvst[i] = kvacc[...].astype(BF16)
        for r in range(1, SUBS):
            kvp_copy(i, r).start()

        def take(n, core, sides):
            query_sum, square_sum = 0.0, 0.0
            for r in sides:
                scaled, query, squares = absorb(sub_at(r) * tps + core, n)
                query_sum, square_sum = query_sum + query, square_sum + squares
            qacc[...] += query_sum
            sumsq[...] += square_sum

        def across(n):
            @pl.when(layer > 0)
            def _():
                for m in range(group):
                    ci = n * group + m
                    for r in (1, 2):
                        wait_block(i, sub_at(r) * tps + t, ci)
                    hop_copy(i, ci).start()
                    for r in (1, 2):
                        for e in range(1, tps):
                            fwd_copy(i, r, ci, e).start()
            take(n, t, (1, 2))
        loop(chunks // group, across)

        def far(n, sides):
            for e in range(1, tps):
                @pl.when(layer > 0)
                def _():
                    for m in range(group):
                        for r in sides:
                            wait_block(i, sub_at(r) * tps + tp_at(e), n * group + m)
                take(n, tp_at(e), sides)
        loop(chunks // group, lambda n: far(n, (1, 2)))

        def diagonal(n):
            @pl.when(layer > 0)
            def _():
                for m in range(group):
                    ci = n * group + m
                    wait_block(i, sub_at(3) * tps + t, ci)
                    for e in range(1, tps):
                        fwd_copy(i, 3, ci, e).start()
            take(n, t, (3,))
        loop(chunks // group, diagonal)
        loop(chunks // group, lambda n: far(n, (3,)))

        scale = lax.rsqrt(jnp.sum(sumsq[...], axis=1, keepdims=True) / depth + NORM_EPS)
        kv = kvacc[...]
        for r in range(1, SUBS):
            kvp_copy(i, r).wait_recv()
            kv = kv + kvrecv[i, r - 1].astype(F32)
        kv = kv * scale
        kvb[i + 1, :, :HEAD_DIM] = rotate(kv[:, :HEAD_DIM], i).astype(BF16)
        kvb[i + 1, :, HEAD_DIM:] = kv[:, HEAD_DIM:].astype(BF16)
        both = jnp.concatenate([kvb[i], kvb[i + 1]], axis=0)
        for g in range(att.shape[1] // HEAD_DIM):
            cols = slice(g * HEAD_DIM, (g + 1) * HEAD_DIM)
            query = rotate(qacc[:, cols] * scale, i).astype(BF16)
            scores = lax.dot_general(
                query, both[:, :HEAD_DIM], (((1,), (1,)), ((), ())), preferred_element_type=F32
            ) * (1.0 / math.sqrt(HEAD_DIM))
            weights = jnp.where(mask[i] > 0.0, jnp.exp(scores), 0.0)
            probs = (weights / jnp.sum(weights, axis=1, keepdims=True)).astype(BF16)
            att[:, cols] = dot(probs, both[:, HEAD_DIM:]).astype(BF16)

        def term(p, ci):
            cols = pl.ds(pl.multiple_of((p * chunks + ci) * block, block), block)
            return dot(att[...], wo[:, cols]).astype(BF16)

        def project(k):
            @pl.when(k < chunks)
            def _():
                for e in range(1, tps):
                    for r in (3, 1, 2, 0):
                        s1out[i, r, k, e - 1] = term(sub_at(r) * tps + tp_at(e), k)
                    for r in (3, 1, 2, 0):
                        s1_copy(i, r, k, e).start()
                for r in range(SUBS):
                    s1own[i, r, k] = term(sub_at(r) * tps + t, k)

            @pl.when((k >= 1) & (k <= chunks))
            def _():
                ci = k - 1
                for r in (3, 1, 2, 0):
                    total = s1own[i, r, ci].astype(F32)
                    for e in range(1, tps):
                        s1_copy(i, r, ci, e).wait_recv()
                        total = total + s1in[i, r, ci, e - 1].astype(F32)
                    s1own[i, r, ci] = total.astype(BF16)
                    if r == 3:
                        cross_copy(i, ci).start()
                s2_copy(i, ci % 2, ci).start()

            @pl.when(k >= 2)
            def _():
                ci = k - 2
                cross_copy(i, ci).wait_recv()
                r = 2 - ci % 2
                passed = s1own[i, r, ci].astype(F32) + s2in[i, 2, ci].astype(F32)
                s1own[i, r, ci] = passed.astype(BF16)
                s2_copy(i, 1 - ci % 2, ci).start()
        loop(chunks + 2, project)

        @pl.when(i == splits - 1)
        def _():
            def deliver(j):
                rows = dot(pick[j, 0], kvb[1])
                for n in range(1, splits):
                    rows = rows + dot(pick[j, n], kvb[n + 1])
                pickst[j] = rows.astype(BF16)

                @pl.when(j == layer)
                def _():
                    kvbuf[layer] = pickst[j]

                @pl.when(j != layer)
                def _():
                    pick_copy(j).start()
            loop(layers, deliver)

        def finish(ci):
            @pl.when(ci < chunks)
            def _():
                terms = s1own[i, 0, ci].astype(F32)
                for which in (0, 1):
                    s2_copy(i, which, ci).wait_recv()
                    terms = terms + s2in[i, which, ci].astype(F32)
                total = hbuf[i, own, ci].astype(F32) + terms

                @pl.when(layer < last)
                def _():
                    upd[i, ci] = total.astype(BF16)
                    z_copy(i, ci).start()

                @pl.when(layer == last)
                def _():
                    totf[:span] = total
                    for n in range(per_split):
                        rows = totf[n * own_tokens:n * own_tokens + fst.shape[2]]
                        fst[i * per_split + n, ci] = rows.astype(BF16)

            @pl.when((ci >= 1) & (layer > 0) & (i < splits - 1))
            def _():
                spread(i + 1, ci - 1)
        loop(chunks + 1, finish)

        @pl.when(layer == last)
        def _():
            def out(n):
                s = i * per_split + n
                mine = (s == section) & (out_tp == t)

                @pl.when(mine)
                def _():
                    fin[out_slot] = fst[s]

                @pl.when(jnp.logical_not(mine))
                def _():
                    fin_copy(s).start()
            loop(per_split, out)

    loop(splits, stage)

    def kv_in(j):
        @pl.when(j != layer)
        def _():
            copy(pickst.at[j], kvbuf.at[j], pk_s.at[j], pk_r.at[j], j * SUBS + u, t).wait_recv()
    loop(layers, kv_in)
    kv_out[...] = kvbuf[...]

    def fin_in(j):
        p = t * SUBS + j
        sec, core = last * SUBS + p // tps, p % tps

        @pl.when((sec != section) | (core != t))
        def _():
            copy(fst.at[0], fin.at[j], fin_s.at[0], fin_r.at[j], sec, core).wait_recv()
    loop(SUBS, fin_in)
    fin_out[...] = fin[...]

    @pl.when(layer == 0)
    def _():
        def sent(k):
            for e in range(1, tps):
                first_copy(k // (SUBS * chunks), k // chunks % SUBS, k % chunks, e).wait_send()
        loop(splits * SUBS * chunks, sent)

    @pl.when(layer > 0)
    def _():
        def sent(k):
            i, ci = k // chunks, k % chunks
            for r in range(SUBS):
                for e in range(1, tps):
                    fwd_copy(i, r, ci, e).wait_send()
            for r in (1, 2):
                ag_copy(i, r, ci).wait_send()
            hop_copy(i, ci).wait_send()
        loop(splits * chunks, sent)

    def kvp_sent(i):
        for r in range(1, SUBS):
            kvp_copy(i, r).wait_send()
    loop(splits, kvp_sent)

    def sums_sent(k):
        i, ci = k // chunks, k % chunks
        for r in range(SUBS):
            for e in range(1, tps):
                s1_copy(i, r, ci, e).wait_send()
        for which in (0, 1):
            s2_copy(i, which, ci).wait_send()
        cross_copy(i, ci).wait_send()

        @pl.when(layer < last)
        def _():
            z_copy(i, ci).wait_send()
    loop(splits * chunks, sums_sent)

    def kv_sent(j):
        @pl.when(j != layer)
        def _():
            pick_copy(j).wait_send()
    loop(layers, kv_sent)

    @pl.when(layer == last)
    def _():
        def sent(s):
            @pl.when(jnp.logical_not((s == section) & (out_tp == t)))
            def _():
                fin_copy(s).wait_send()
        loop(sections, sent)


def shards(
    hidden_t, norm_gain, q_weight, k_weight, v_weight, o_weight, lengths, prior_offsets, owners
):
    sections = lax.axis_size("section")
    tps = lax.axis_size("tp")
    section = lax.axis_index("section")
    layers = sections // SUBS
    layer = section // SUBS
    sub = section % SUBS
    rows_dev, tokens = hidden_t.shape
    num_reqs = lengths.shape[0]
    capacity = 2 * tokens // num_reqs
    cap_pad = round_up(capacity, 16)
    own_tokens = tokens // sections
    tok_pad = round_up(own_tokens, 16)
    pieces = SUBS * tps
    block = min(BLOCK, rows_dev // SUBS)
    chunks = rows_dev // SUBS // block
    q_cols = q_weight.shape[2]
    span = tokens // SPLIT
    assert span >= capacity and sections % SPLIT == 0 and span % 16 == 0

    req_ends = jnp.cumsum(lengths)
    req_starts = req_ends - lengths
    tok_ids = jnp.arange(tokens, dtype=jnp.int32)
    req_ids = jnp.arange(num_reqs, dtype=jnp.int32)
    req_of_tok = jnp.sum((tok_ids[:, None] >= req_ends[None, :]).astype(jnp.int32), axis=1)
    req_onehot = req_of_tok[:, None] == req_ids[None, :]
    positions = (
        jnp.sum(jnp.where(req_onehot, (prior_offsets - req_starts)[None, :], 0), axis=1) + tok_ids
    )
    spans = jnp.arange(SPLIT, dtype=jnp.int32)[:, None, None] * span
    query_ids = spans + jnp.arange(span, dtype=jnp.int32)[None, :, None]
    key_ids = spans + jnp.arange(-span, span, dtype=jnp.int32)[None, None, :]
    first_ids = jnp.sum(jnp.where(req_onehot, req_starts[None, :], 0), axis=1).reshape(SPLIT, span, 1)
    mask = ((key_ids >= first_ids) & (key_ids <= query_ids)).astype(F32)
    half = HEAD_DIM // 2
    inv_freq = jnp.power(F32(ROPE_BASE), -(2.0 * jnp.arange(half, dtype=F32)) / HEAD_DIM)
    angle = positions.astype(F32)[:, None] * inv_freq[None, :]
    cos, sin = jnp.cos(angle), jnp.sin(angle)
    cosf = jnp.concatenate([cos, cos], axis=1).reshape(SPLIT, span, HEAD_DIM)
    sinf = jnp.concatenate([-sin, sin], axis=1).reshape(SPLIT, span, HEAD_DIM)

    mine = jnp.arange(layers, dtype=jnp.int32) * SUBS + sub
    chosen = owners[None, :] == mine[:, None]
    start = jnp.sum(jnp.where(chosen, req_starts[None, :], 0), axis=1)
    count = jnp.sum(jnp.where(chosen, lengths[None, :], 0), axis=1)
    slots = jnp.arange(cap_pad, dtype=jnp.int32)
    tok_split = tok_ids.reshape(1, SPLIT, 1, span)
    slots = slots[None, None, :, None]
    pick = (
        (tok_split == start[:, None, None, None] + slots) & (slots < count[:, None, None, None])
    ).astype(BF16)

    gain = lax.dynamic_index_in_dim(norm_gain, layer, 0, keepdims=False).astype(F32)
    gain = gain.reshape(pieces * chunks, 1, block)

    vm = pltpu.VMEM
    dma = pltpu.SemaphoreType.DMA
    others = tps - 1
    far_subs = SUBS - 1
    blk = (span, block)
    kv_cols = 2 * HEAD_DIM
    fin, kv = pl.pallas_call(
        functools.partial(relay_kernel, layers, tps, own_tokens),
        out_shape=(
            jax.ShapeDtypeStruct((SUBS, chunks, tok_pad, block), BF16),
            jax.ShapeDtypeStruct((layers, cap_pad, 2 * HEAD_DIM), BF16),
        ),
        in_specs=[pl.BlockSpec(memory_space=pltpu.VMEM)] * 10,
        out_specs=(pl.BlockSpec(memory_space=pltpu.VMEM),) * 2,
        scratch_shapes=[
            vm((SPLIT, pieces, chunks) + blk, BF16),
            vm((span, q_cols), F32),
            vm((span, kv_cols), F32),
            vm((span, HEAD_DIM), F32),
            vm((SPLIT, span, kv_cols), BF16),
            vm((SPLIT, far_subs, span, kv_cols), BF16),
            vm((SPLIT + 1, span, kv_cols), BF16),
            vm((span, q_cols), BF16),
            vm((SPLIT, SUBS, chunks, others) + blk, BF16),
            vm((SPLIT, SUBS, chunks, others) + blk, BF16),
            vm((SPLIT, SUBS, chunks) + blk, BF16),
            vm((SPLIT, far_subs, chunks) + blk, BF16),
            vm((SPLIT, chunks) + blk, BF16),
            vm((span + 32, block), F32),
            vm((sections, chunks, tok_pad, block), BF16),
            vm((SUBS, chunks, tok_pad, block), BF16),
            vm((layers, cap_pad, 2 * HEAD_DIM), BF16),
            vm((layers, cap_pad, 2 * HEAD_DIM), BF16),
            dma((SPLIT, pieces, chunks)),
            dma((SPLIT, SUBS, chunks, others)),
            dma((SPLIT, far_subs, chunks)),
            dma((SPLIT, far_subs)),
            dma((SPLIT, far_subs)),
            dma((SPLIT, SUBS, chunks, others)),
            dma((SPLIT, SUBS, chunks, others)),
            dma((SPLIT, far_subs, chunks)),
            dma((SPLIT, far_subs, chunks)),
            dma((SPLIT, chunks)),
            dma((layers,)),
            dma((layers,)),
            dma((sections,)),
            dma((SUBS,)),
        ],
        compiler_params=pltpu.CompilerParams(
            collective_id=0, has_side_effects=True, vmem_limit_bytes=56 * 1024 * 1024
        ),
        name="relay",
    )(hidden_t, gain, q_weight[0], k_weight[0], v_weight[0], o_weight[0], cosf, sinf, mask, pick)
    final_hidden = fin[:, :, :own_tokens].transpose(0, 1, 3, 2).reshape(rows_dev, own_tokens)
    return final_hidden, kv[None, :, :capacity]


def solution(mesh):
    return jax.shard_map(
        shards,
        mesh=mesh,
        in_specs=(
            P("tp", None),
            P(),
            P("section", None, "tp"),
            P("section", None, "tp"),
            P("section", None, "tp"),
            P("section", "tp", None),
            P(),
            P(),
            P(),
        ),
        out_specs=(P("tp", "section"), P("section", None, None, "tp")),
        check_vma=False,
    )
```

```python
import functools
import math

import jax
import jax.numpy as jnp
from jax import lax
from jax.experimental import pallas as pl
from jax.experimental.pallas import tpu as pltpu
from jax.sharding import PartitionSpec as P

HEAD_DIM = 128
SUBS = 4
BLOCK = 512
GROUP = 1
SPLIT = 4
NORM_EPS = 1e-05
ROPE_BASE = 500000.0
MESH = pl.DeviceIdType.MESH
F32 = jnp.float32
BF16 = jnp.bfloat16


def dot(a, b):
    return jnp.dot(a, b, preferred_element_type=F32)


def round_up(count, unit):
    return (count + unit - 1) // unit * unit


def relay_kernel(
    layers, tps, own_tokens,
    hin, gain, wq, wk, wv, wo, cosf, sinf, mask, pick,
    fin_out, kv_out,
    hbuf, qacc, kvacc, sumsq, kvst, kvrecv, kvb, att,
    s1out, s1in, s1own, s2in, upd, totf, fst, fin, pickst, kvbuf,
    hs, fwd_s, ag_s, kvp_s, kvp_r, s1_s, s1_r, s2_s, s2_r, z_s, pk_s, pk_r, fin_s, fin_r,
):
    section = lax.axis_index("section")
    t = lax.axis_index("tp")
    layer = section // SUBS
    u = section % SUBS
    splits, pieces, chunks, span, block = hbuf.shape
    depth = pieces * chunks * block
    group = min(GROUP, chunks)
    per_split = layers * SUBS // splits
    own = u * tps + t
    sections = layers * SUBS
    last = layers - 1
    out_tp = own // SUBS
    out_slot = own % SUBS
    base = layer * SUBS

    def copy(src, dst, send, recv, sec, core):
        return pltpu.make_async_remote_copy(
            src_ref=src, dst_ref=dst, send_sem=send, recv_sem=recv,
            device_id=(sec, core), device_id_type=MESH,
        )

    def sub_at(r):
        return (u + r) % SUBS

    def tp_at(e):
        return (t + e) % tps

    def first_copy(i, j, ci, e):
        p = t * SUBS + j
        return copy(hbuf.at[i, p, ci], hbuf.at[i, p, ci], fwd_s.at[i, j, ci, e - 1], hs.at[i, p, ci],
                    section, tp_at(e))

    def fwd_copy(i, r, ci, e):
        p = sub_at(r) * tps + t
        return copy(hbuf.at[i, p, ci], hbuf.at[i, p, ci], fwd_s.at[i, r, ci, e - 1], hs.at[i, p, ci],
                    section, tp_at(e))

    def ag_copy(i, r, ci):
        return copy(hbuf.at[i, own, ci], hbuf.at[i, own, ci], ag_s.at[i, r - 1, ci], hs.at[i, own, ci],
                    base + sub_at(r), t)

    def wait_block(i, p, ci):
        copy(hbuf.at[i, p, ci], hbuf.at[i, p, ci], fwd_s.at[0, 0, 0, 0], hs.at[i, p, ci],
             section, tp_at(1)).wait_recv()

    def kvp_copy(i, r):
        return copy(kvst.at[i], kvrecv.at[i, r - 1], kvp_s.at[i, r - 1], kvp_r.at[i, r - 1],
                    base + sub_at(r), t)

    def s1_copy(i, r, ci, e):
        return copy(s1out.at[i, r, ci, e - 1], s1in.at[i, r, ci, e - 1], s1_s.at[i, r, ci, e - 1],
                    s1_r.at[i, r, ci, e - 1], section, tp_at(e))

    def s2_copy(i, r, ci):
        return copy(s1own.at[i, r, ci], s2in.at[i, r - 1, ci], s2_s.at[i, r - 1, ci], s2_r.at[i, r - 1, ci],
                    base + sub_at(r), t)

    def z_copy(i, ci):
        return copy(upd.at[i, ci], hbuf.at[i, own, ci], z_s.at[i, ci], hs.at[i, own, ci], section + SUBS, t)

    def pick_copy(j):
        return copy(pickst.at[j], kvbuf.at[layer], pk_s.at[j], pk_r.at[layer], j * SUBS + u, t)

    def fin_copy(s):
        return copy(fst.at[s], fin.at[out_slot], fin_s.at[s], fin_r.at[out_slot], s, out_tp)

    def loop(count, body):
        def step(k, carry):
            body(k)
            return carry
        lax.fori_loop(0, count, step, jnp.int32(0))

    barrier = pltpu.get_barrier_semaphore()

    def greet(sec, core):
        pl.semaphore_signal(barrier, inc=1, device_id=(sec, core), device_id_type=MESH)

    for e in range(1, tps):
        greet(section, tp_at(e))
    for r in range(1, SUBS):
        greet(base + sub_at(r), t)
    for j in range(1, layers):
        greet((layer + j) % layers * SUBS + u, t)
    for j in range(SUBS):
        p = t * SUBS + j
        sec, core = last * SUBS + p // tps, p % tps

        @pl.when((sec != section) | (core != t))
        def _():
            greet(sec, core)

    spread_to = jnp.where(layer == last, sections - jnp.where(out_tp == t, 1, 0), 0)
    pl.semaphore_wait(barrier, (tps - 1) + (SUBS - 1) + (layers - 1) + spread_to)

    totf[...] = jnp.zeros_like(totf)
    kvb[0] = jnp.zeros_like(kvb[0])

    @pl.when(layer == 0)
    def _():
        def send(k):
            j, ci = k // chunks, k % chunks
            rows = pl.ds(pl.multiple_of(k * block, block), block)
            turned = hin[rows, :].astype(F32).T.astype(BF16)
            for i in range(splits):
                hbuf[i, t * SUBS + j, ci] = turned[i * span:(i + 1) * span]
                for e in range(1, tps):
                    first_copy(i, j, ci, e).start()
        loop(SUBS * chunks, send)

    def spread(i, ci):
        wait_block(i, own, ci)
        for r in range(1, SUBS):
            ag_copy(i, r, ci).start()
        for e in range(1, tps):
            fwd_copy(i, 0, ci, e).start()

    def rotate(x, i):
        return x * cosf[i] + pltpu.roll(x, HEAD_DIM // 2, 1) * sinf[i]

    def stage(i):
        qacc[...] = jnp.zeros_like(qacc)
        kvacc[...] = jnp.zeros_like(kvacc)
        sumsq[...] = jnp.zeros_like(sumsq)

        @pl.when(layer == 0)
        def _():
            def arrive(k):
                j, ci = k // chunks, k % chunks
                for e in range(1, tps):
                    wait_block(i, tp_at(e) * SUBS + j, ci)
            loop(SUBS * chunks, arrive)

        @pl.when((layer > 0) & (i == 0))
        def _():
            loop(chunks, lambda ci: spread(0, ci))

        def absorb(p, n):
            parts, squares = [], 0.0
            for m in range(group):
                ci = n * group + m
                x = hbuf[i, p, ci].astype(F32)
                sq = x * x
                for w in range(block // HEAD_DIM):
                    squares = squares + sq[:, w * HEAD_DIM:(w + 1) * HEAD_DIM]
                parts.append((x * gain[p * chunks + ci]).astype(BF16))
            scaled = jnp.concatenate(parts, axis=1)
            width = group * block
            rows = pl.ds(pl.multiple_of(p * chunks * block + n * width, width), width)
            return scaled, dot(scaled, wq[rows, :]), squares

        def near(n):
            for m in range(group):
                for e in range(1, tps):
                    @pl.when(layer > 0)
                    def _():
                        wait_block(i, u * tps + tp_at(e), n * group + m)
            query_sum, square_sum, kv_sum = 0.0, 0.0, 0.0
            width = group * block
            for e in range(tps):
                d = tp_at(e)
                scaled, query, squares = absorb(u * tps + d, n)
                query_sum, square_sum = query_sum + query, square_sum + squares
                rows = pl.ds(pl.multiple_of(d * chunks * block + n * width, width), width)
                kv_sum = kv_sum + dot(scaled, jnp.concatenate([wk[rows, :], wv[rows, :]], axis=1))
            qacc[...] += query_sum
            sumsq[...] += square_sum
            kvacc[...] += kv_sum
        loop(chunks // group, near)

        kvst[i] = kvacc[...].astype(BF16)
        for r in range(1, SUBS):
            kvp_copy(i, r).start()

        def take(n, core):
            query_sum, square_sum = 0.0, 0.0
            for r in range(1, SUBS):
                scaled, query, squares = absorb(sub_at(r) * tps + core, n)
                query_sum, square_sum = query_sum + query, square_sum + squares
            qacc[...] += query_sum
            sumsq[...] += square_sum

        def across(n):
            @pl.when(layer > 0)
            def _():
                for m in range(group):
                    for r in range(1, SUBS):
                        ci = n * group + m
                        wait_block(i, sub_at(r) * tps + t, ci)
                        for e in range(1, tps):
                            fwd_copy(i, r, ci, e).start()
            take(n, t)
        loop(chunks // group, across)

        def far(n):
            for e in range(1, tps):
                @pl.when(layer > 0)
                def _():
                    for m in range(group):
                        for r in range(1, SUBS):
                            wait_block(i, sub_at(r) * tps + tp_at(e), n * group + m)
                take(n, tp_at(e))
        loop(chunks // group, far)

        scale = lax.rsqrt(jnp.sum(sumsq[...], axis=1, keepdims=True) / depth + NORM_EPS)
        kv = kvacc[...]
        for r in range(1, SUBS):
            kvp_copy(i, r).wait_recv()
            kv = kv + kvrecv[i, r - 1].astype(F32)
        kv = kv * scale
        kvb[i + 1, :, :HEAD_DIM] = rotate(kv[:, :HEAD_DIM], i).astype(BF16)
        kvb[i + 1, :, HEAD_DIM:] = kv[:, HEAD_DIM:].astype(BF16)
        both = jnp.concatenate([kvb[i], kvb[i + 1]], axis=0)
        for g in range(att.shape[1] // HEAD_DIM):
            cols = slice(g * HEAD_DIM, (g + 1) * HEAD_DIM)
            query = rotate(qacc[:, cols] * scale, i).astype(BF16)
            scores = lax.dot_general(
                query, both[:, :HEAD_DIM], (((1,), (1,)), ((), ())), preferred_element_type=F32
            ) * (1.0 / math.sqrt(HEAD_DIM))
            weights = jnp.where(mask[i] > 0.0, jnp.exp(scores), 0.0)
            probs = (weights / jnp.sum(weights, axis=1, keepdims=True)).astype(BF16)
            att[:, cols] = dot(probs, both[:, HEAD_DIM:]).astype(BF16)

        def term(p, ci):
            cols = pl.ds(pl.multiple_of((p * chunks + ci) * block, block), block)
            return dot(att[...], wo[:, cols]).astype(BF16)

        def project(k):
            @pl.when(k < chunks)
            def _():
                for e in range(1, tps):
                    for r in (1, 2, 3, 0):
                        s1out[i, r, k, e - 1] = term(sub_at(r) * tps + tp_at(e), k)
                    for r in (1, 2, 3, 0):
                        s1_copy(i, r, k, e).start()
                for r in range(SUBS):
                    s1own[i, r, k] = term(sub_at(r) * tps + t, k)

            @pl.when(k >= 1)
            def _():
                ci = k - 1
                for r in (1, 2, 3, 0):
                    total = s1own[i, r, ci].astype(F32)
                    for e in range(1, tps):
                        s1_copy(i, r, ci, e).wait_recv()
                        total = total + s1in[i, r, ci, e - 1].astype(F32)
                    s1own[i, r, ci] = total.astype(BF16)
                    if r > 0:
                        s2_copy(i, r, ci).start()
        loop(chunks + 1, project)

        @pl.when(i == splits - 1)
        def _():
            def deliver(j):
                rows = dot(pick[j, 0], kvb[1])
                for n in range(1, splits):
                    rows = rows + dot(pick[j, n], kvb[n + 1])
                pickst[j] = rows.astype(BF16)

                @pl.when(j == layer)
                def _():
                    kvbuf[layer] = pickst[j]

                @pl.when(j != layer)
                def _():
                    pick_copy(j).start()
            loop(layers, deliver)

        def finish(ci):
            @pl.when(ci < chunks)
            def _():
                terms = s1own[i, 0, ci].astype(F32)
                for r in range(1, SUBS):
                    s2_copy(i, r, ci).wait_recv()
                    terms = terms + s2in[i, r - 1, ci].astype(F32)
                total = hbuf[i, own, ci].astype(F32) + terms

                @pl.when(layer < last)
                def _():
                    upd[i, ci] = total.astype(BF16)
                    z_copy(i, ci).start()

                @pl.when(layer == last)
                def _():
                    totf[:span] = total
                    for n in range(per_split):
                        rows = totf[n * own_tokens:n * own_tokens + fst.shape[2]]
                        fst[i * per_split + n, ci] = rows.astype(BF16)

            @pl.when((ci >= 1) & (layer > 0) & (i < splits - 1))
            def _():
                spread(i + 1, ci - 1)
        loop(chunks + 1, finish)

        @pl.when(layer == last)
        def _():
            def out(n):
                s = i * per_split + n
                mine = (s == section) & (out_tp == t)

                @pl.when(mine)
                def _():
                    fin[out_slot] = fst[s]

                @pl.when(jnp.logical_not(mine))
                def _():
                    fin_copy(s).start()
            loop(per_split, out)

    loop(splits, stage)

    def kv_in(j):
        @pl.when(j != layer)
        def _():
            copy(pickst.at[j], kvbuf.at[j], pk_s.at[j], pk_r.at[j], j * SUBS + u, t).wait_recv()
    loop(layers, kv_in)
    kv_out[...] = kvbuf[...]

    def fin_in(j):
        p = t * SUBS + j
        sec, core = last * SUBS + p // tps, p % tps

        @pl.when((sec != section) | (core != t))
        def _():
            copy(fst.at[0], fin.at[j], fin_s.at[0], fin_r.at[j], sec, core).wait_recv()
    loop(SUBS, fin_in)
    fin_out[...] = fin[...]

    @pl.when(layer == 0)
    def _():
        def sent(k):
            for e in range(1, tps):
                first_copy(k // (SUBS * chunks), k // chunks % SUBS, k % chunks, e).wait_send()
        loop(splits * SUBS * chunks, sent)

    @pl.when(layer > 0)
    def _():
        def sent(k):
            i, ci = k // chunks, k % chunks
            for r in range(SUBS):
                for e in range(1, tps):
                    fwd_copy(i, r, ci, e).wait_send()
            for r in range(1, SUBS):
                ag_copy(i, r, ci).wait_send()
        loop(splits * chunks, sent)

    def kvp_sent(i):
        for r in range(1, SUBS):
            kvp_copy(i, r).wait_send()
    loop(splits, kvp_sent)

    def sums_sent(k):
        i, ci = k // chunks, k % chunks
        for r in range(SUBS):
            for e in range(1, tps):
                s1_copy(i, r, ci, e).wait_send()
        for r in range(1, SUBS):
            s2_copy(i, r, ci).wait_send()

        @pl.when(layer < last)
        def _():
            z_copy(i, ci).wait_send()
    loop(splits * chunks, sums_sent)

    def kv_sent(j):
        @pl.when(j != layer)
        def _():
            pick_copy(j).wait_send()
    loop(layers, kv_sent)

    @pl.when(layer == last)
    def _():
        def sent(s):
            @pl.when(jnp.logical_not((s == section) & (out_tp == t)))
            def _():
                fin_copy(s).wait_send()
        loop(sections, sent)


def shards(
    hidden_t, norm_gain, q_weight, k_weight, v_weight, o_weight, lengths, prior_offsets, owners
):
    sections = lax.axis_size("section")
    tps = lax.axis_size("tp")
    section = lax.axis_index("section")
    layers = sections // SUBS
    layer = section // SUBS
    sub = section % SUBS
    rows_dev, tokens = hidden_t.shape
    num_reqs = lengths.shape[0]
    capacity = 2 * tokens // num_reqs
    cap_pad = round_up(capacity, 16)
    own_tokens = tokens // sections
    tok_pad = round_up(own_tokens, 16)
    pieces = SUBS * tps
    block = min(BLOCK, rows_dev // SUBS)
    chunks = rows_dev // SUBS // block
    q_cols = q_weight.shape[2]
    span = tokens // SPLIT
    assert span >= capacity and sections % SPLIT == 0 and span % 16 == 0

    req_ends = jnp.cumsum(lengths)
    req_starts = req_ends - lengths
    tok_ids = jnp.arange(tokens, dtype=jnp.int32)
    req_ids = jnp.arange(num_reqs, dtype=jnp.int32)
    req_of_tok = jnp.sum((tok_ids[:, None] >= req_ends[None, :]).astype(jnp.int32), axis=1)
    req_onehot = req_of_tok[:, None] == req_ids[None, :]
    positions = (
        jnp.sum(jnp.where(req_onehot, (prior_offsets - req_starts)[None, :], 0), axis=1) + tok_ids
    )
    spans = jnp.arange(SPLIT, dtype=jnp.int32)[:, None, None] * span
    query_ids = spans + jnp.arange(span, dtype=jnp.int32)[None, :, None]
    key_ids = spans + jnp.arange(-span, span, dtype=jnp.int32)[None, None, :]
    first_ids = jnp.sum(jnp.where(req_onehot, req_starts[None, :], 0), axis=1).reshape(SPLIT, span, 1)
    mask = ((key_ids >= first_ids) & (key_ids <= query_ids)).astype(F32)
    half = HEAD_DIM // 2
    inv_freq = jnp.power(F32(ROPE_BASE), -(2.0 * jnp.arange(half, dtype=F32)) / HEAD_DIM)
    angle = positions.astype(F32)[:, None] * inv_freq[None, :]
    cos, sin = jnp.cos(angle), jnp.sin(angle)
    cosf = jnp.concatenate([cos, cos], axis=1).reshape(SPLIT, span, HEAD_DIM)
    sinf = jnp.concatenate([-sin, sin], axis=1).reshape(SPLIT, span, HEAD_DIM)

    mine = jnp.arange(layers, dtype=jnp.int32) * SUBS + sub
    chosen = owners[None, :] == mine[:, None]
    start = jnp.sum(jnp.where(chosen, req_starts[None, :], 0), axis=1)
    count = jnp.sum(jnp.where(chosen, lengths[None, :], 0), axis=1)
    slots = jnp.arange(cap_pad, dtype=jnp.int32)
    tok_split = tok_ids.reshape(1, SPLIT, 1, span)
    slots = slots[None, None, :, None]
    pick = (
        (tok_split == start[:, None, None, None] + slots) & (slots < count[:, None, None, None])
    ).astype(BF16)

    gain = lax.dynamic_index_in_dim(norm_gain, layer, 0, keepdims=False).astype(F32)
    gain = gain.reshape(pieces * chunks, 1, block)

    vm = pltpu.VMEM
    dma = pltpu.SemaphoreType.DMA
    others = tps - 1
    far_subs = SUBS - 1
    blk = (span, block)
    kv_cols = 2 * HEAD_DIM
    fin, kv = pl.pallas_call(
        functools.partial(relay_kernel, layers, tps, own_tokens),
        out_shape=(
            jax.ShapeDtypeStruct((SUBS, chunks, tok_pad, block), BF16),
            jax.ShapeDtypeStruct((layers, cap_pad, 2 * HEAD_DIM), BF16),
        ),
        in_specs=[pl.BlockSpec(memory_space=pltpu.VMEM)] * 10,
        out_specs=(pl.BlockSpec(memory_space=pltpu.VMEM),) * 2,
        scratch_shapes=[
            vm((SPLIT, pieces, chunks) + blk, BF16),
            vm((span, q_cols), F32),
            vm((span, kv_cols), F32),
            vm((span, HEAD_DIM), F32),
            vm((SPLIT, span, kv_cols), BF16),
            vm((SPLIT, far_subs, span, kv_cols), BF16),
            vm((SPLIT + 1, span, kv_cols), BF16),
            vm((span, q_cols), BF16),
            vm((SPLIT, SUBS, chunks, others) + blk, BF16),
            vm((SPLIT, SUBS, chunks, others) + blk, BF16),
            vm((SPLIT, SUBS, chunks) + blk, BF16),
            vm((SPLIT, far_subs, chunks) + blk, BF16),
            vm((SPLIT, chunks) + blk, BF16),
            vm((span + 32, block), F32),
            vm((sections, chunks, tok_pad, block), BF16),
            vm((SUBS, chunks, tok_pad, block), BF16),
            vm((layers, cap_pad, 2 * HEAD_DIM), BF16),
            vm((layers, cap_pad, 2 * HEAD_DIM), BF16),
            dma((SPLIT, pieces, chunks)),
            dma((SPLIT, SUBS, chunks, others)),
            dma((SPLIT, far_subs, chunks)),
            dma((SPLIT, far_subs)),
            dma((SPLIT, far_subs)),
            dma((SPLIT, SUBS, chunks, others)),
            dma((SPLIT, SUBS, chunks, others)),
            dma((SPLIT, far_subs, chunks)),
            dma((SPLIT, far_subs, chunks)),
            dma((SPLIT, chunks)),
            dma((layers,)),
            dma((layers,)),
            dma((sections,)),
            dma((SUBS,)),
        ],
        compiler_params=pltpu.CompilerParams(
            collective_id=0, has_side_effects=True, vmem_limit_bytes=56 * 1024 * 1024
        ),
        name="relay",
    )(hidden_t, gain, q_weight[0], k_weight[0], v_weight[0], o_weight[0], cosf, sinf, mask, pick)
    final_hidden = fin[:, :, :own_tokens].transpose(0, 1, 3, 2).reshape(rows_dev, own_tokens)
    return final_hidden, kv[None, :, :capacity]


def solution(mesh):
    return jax.shard_map(
        shards,
        mesh=mesh,
        in_specs=(
            P("tp", None),
            P(),
            P("section", None, "tp"),
            P("section", None, "tp"),
            P("section", None, "tp"),
            P("section", "tp", None),
            P(),
            P(),
            P(),
        ),
        out_specs=(P("tp", "section"), P("section", None, None, "tp")),
        check_vma=False,
    )
```

```python
import functools
import math

import jax
import jax.numpy as jnp
from jax import lax
from jax.experimental import pallas as pl
from jax.experimental.pallas import tpu as pltpu
from jax.sharding import PartitionSpec as P

HEAD_DIM = 128
SUBS = 4
BLOCK = 256
GROUP = 2
SPLIT = 4
NORM_EPS = 1e-05
ROPE_BASE = 500000.0
MESH = pl.DeviceIdType.MESH
F32 = jnp.float32
BF16 = jnp.bfloat16


def dot(a, b):
    return jnp.dot(a, b, preferred_element_type=F32)


def round_up(count, unit):
    return (count + unit - 1) // unit * unit


def relay_kernel(
    layers, tps, own_tokens,
    hin_hbm, wq_hbm, wk_hbm, wv_hbm, wo_hbm, gain, cosf, sinf, first, pick,
    fin_out, kv_out,
    hbuf, qacc, kvacc, sumsq, kvst, kvrecv, kvb, att,
    s1out, s1in, s1own, s2in, upd, totf, fst, fin, pickst, kvbuf,
    hs, fwd_s, ag_s, kvp_s, kvp_r, s1_s, s1_r, s2_s, s2_r, z_s, pk_s, pk_r, fin_s, fin_r,
    hin, wq, wk, wv, wo, load_s,
):
    section = lax.axis_index("section")
    t = lax.axis_index("tp")
    layer = section // SUBS
    u = section % SUBS
    splits, pieces, chunks, span, block = hbuf.shape
    depth = pieces * chunks * block
    group = min(GROUP, chunks)
    per_split = layers * SUBS // splits
    own = u * tps + t
    sections = layers * SUBS
    last = layers - 1
    out_tp = own // SUBS
    out_slot = own % SUBS
    base = layer * SUBS

    def copy(src, dst, send, recv, sec, core):
        return pltpu.make_async_remote_copy(
            src_ref=src, dst_ref=dst, send_sem=send, recv_sem=recv,
            device_id=(sec, core), device_id_type=MESH,
        )

    def sub_at(r):
        return (u + r) % SUBS

    def tp_at(e):
        return (t + e) % tps

    def first_copy(i, j, ci, e):
        p = t * SUBS + j
        return copy(hbuf.at[i, p, ci], hbuf.at[i, p, ci], fwd_s.at[i, j, ci, e - 1], hs.at[i, p, ci],
                    section, tp_at(e))

    def fwd_copy(i, r, ci, e):
        p = sub_at(r) * tps + t
        return copy(hbuf.at[i, p, ci], hbuf.at[i, p, ci], fwd_s.at[i, r, ci, e - 1], hs.at[i, p, ci],
                    section, tp_at(e))

    def ag_copy(i, r, ci):
        return copy(hbuf.at[i, own, ci], hbuf.at[i, own, ci], ag_s.at[i, r - 1, ci], hs.at[i, own, ci],
                    base + sub_at(r), t)

    def wait_block(i, p, ci):
        copy(hbuf.at[i, p, ci], hbuf.at[i, p, ci], fwd_s.at[0, 0, 0, 0], hs.at[i, p, ci],
             section, tp_at(1)).wait_recv()

    def kvp_copy(i, r):
        return copy(kvst.at[i], kvrecv.at[i, r - 1], kvp_s.at[i, r - 1], kvp_r.at[i, r - 1],
                    base + sub_at(r), t)

    def s1_copy(i, r, ci, e):
        return copy(s1out.at[i, r, ci, e - 1], s1in.at[i, r, ci, e - 1], s1_s.at[i, r, ci, e - 1],
                    s1_r.at[i, r, ci, e - 1], section, tp_at(e))

    def s2_copy(i, r, ci):
        return copy(s1own.at[i, r, ci], s2in.at[i, r - 1, ci], s2_s.at[i, r - 1, ci], s2_r.at[i, r - 1, ci],
                    base + sub_at(r), t)

    def z_copy(i, ci):
        return copy(upd.at[i, ci], hbuf.at[i, own, ci], z_s.at[i, ci], hs.at[i, own, ci], section + SUBS, t)

    def pick_copy(j):
        return copy(pickst.at[j], kvbuf.at[layer], pk_s.at[j], pk_r.at[layer], j * SUBS + u, t)

    def fin_copy(s):
        return copy(fst.at[s], fin.at[out_slot], fin_s.at[s], fin_r.at[out_slot], s, out_tp)

    def loop(count, body):
        def step(k, carry):
            body(k)
            return carry
        lax.fori_loop(0, count, step, jnp.int32(0))

    def load(n, src, dst):
        return pltpu.make_async_copy(src, dst, load_s.at[n])

    in_load = load(0, hin_hbm, hin)
    out_load = load(4, wo_hbm, wo)
    loads = (load(1, wq_hbm, wq), load(2, wk_hbm, wk), load(3, wv_hbm, wv))

    @pl.when(layer == 0)
    def _():
        in_load.start()
    for each in loads:
        each.start()
    out_load.start()

    barrier = pltpu.get_barrier_semaphore()

    def greet(sec, core):
        pl.semaphore_signal(barrier, inc=1, device_id=(sec, core), device_id_type=MESH)

    for e in range(1, tps):
        greet(section, tp_at(e))
    for r in range(1, SUBS):
        greet(base + sub_at(r), t)
    for j in range(1, layers):
        greet((layer + j) % layers * SUBS + u, t)
    for j in range(SUBS):
        p = t * SUBS + j
        sec, core = last * SUBS + p // tps, p % tps

        @pl.when((sec != section) | (core != t))
        def _():
            greet(sec, core)

    spread_to = jnp.where(layer == last, sections - jnp.where(out_tp == t, 1, 0), 0)
    pl.semaphore_wait(barrier, (tps - 1) + (SUBS - 1) + (layers - 1) + spread_to)

    totf[...] = jnp.zeros_like(totf)
    kvb[0] = jnp.zeros_like(kvb[0])

    @pl.when(layer == 0)
    def _():
        in_load.wait()
        wide = round_up(span, HEAD_DIM)

        def send(k):
            j, ci = k // chunks, k % chunks
            rows = pl.ds(pl.multiple_of(k * block, block), block)
            turned = hin[rows, :wide].astype(F32).T.astype(BF16)
            hbuf[0, t * SUBS + j, ci] = turned[:span]
            for e in range(1, tps):
                first_copy(0, j, ci, e).start()
        loop(SUBS * chunks, send)

    def send_rest(k):
        j, ci = k // chunks, k % chunks
        rows = pl.ds(pl.multiple_of(k * block, block), block)
        turned = hin[rows, :].astype(F32).T.astype(BF16)
        for i in range(1, splits):
            hbuf[i, t * SUBS + j, ci] = turned[i * span:(i + 1) * span]
            for e in range(1, tps):
                first_copy(i, j, ci, e).start()

    for each in loads:
        each.wait()

    def spread(i, ci):
        wait_block(i, own, ci)
        for r in range(1, SUBS):
            ag_copy(i, r, ci).start()
        for e in range(1, tps):
            fwd_copy(i, 0, ci, e).start()

    def rotate(x, i):
        return x * cosf[i] + pltpu.roll(x, HEAD_DIM // 2, 1) * sinf[i]

    def stage(i):
        qacc[...] = jnp.zeros_like(qacc)
        kvacc[...] = jnp.zeros_like(kvacc)
        sumsq[...] = jnp.zeros_like(sumsq)

        @pl.when(layer == 0)
        def _():
            def arrive(k):
                j, ci = k // chunks, k % chunks
                for e in range(1, tps):
                    wait_block(i, tp_at(e) * SUBS + j, ci)
            loop(SUBS * chunks, arrive)

        @pl.when((layer > 0) & (i == 0))
        def _():
            loop(chunks, lambda ci: spread(0, ci))

        def absorb(p, n):
            parts, squares = [], 0.0
            for m in range(group):
                ci = n * group + m
                x = hbuf[i, p, ci].astype(F32)
                sq = x * x
                for w in range(block // HEAD_DIM):
                    squares = squares + sq[:, w * HEAD_DIM:(w + 1) * HEAD_DIM]
                parts.append((x * gain[p * chunks + ci]).astype(BF16))
            scaled = jnp.concatenate(parts, axis=1)
            width = group * block
            rows = pl.ds(pl.multiple_of(p * chunks * block + n * width, width), width)
            return scaled, dot(scaled, wq[rows, :]), squares

        def near(n):
            for m in range(group):
                for e in range(1, tps):
                    @pl.when(layer > 0)
                    def _():
                        wait_block(i, u * tps + tp_at(e), n * group + m)
            query_sum, square_sum, kv_sum = 0.0, 0.0, 0.0
            width = group * block
            for e in range(tps):
                d = tp_at(e)
                scaled, query, squares = absorb(u * tps + d, n)
                query_sum, square_sum = query_sum + query, square_sum + squares
                rows = pl.ds(pl.multiple_of(d * chunks * block + n * width, width), width)
                kv_sum = kv_sum + dot(scaled, jnp.concatenate([wk[rows, :], wv[rows, :]], axis=1))
            qacc[...] += query_sum
            sumsq[...] += square_sum
            kvacc[...] += kv_sum
        loop(chunks // group, near)

        kvst[i] = kvacc[...].astype(BF16)
        for r in range(1, SUBS):
            kvp_copy(i, r).start()

        def take(n, core):
            query_sum, square_sum = 0.0, 0.0
            for r in range(1, SUBS):
                scaled, query, squares = absorb(sub_at(r) * tps + core, n)
                query_sum, square_sum = query_sum + query, square_sum + squares
            qacc[...] += query_sum
            sumsq[...] += square_sum

        def across(n):
            @pl.when(layer > 0)
            def _():
                for m in range(group):
                    for r in range(1, SUBS):
                        ci = n * group + m
                        wait_block(i, sub_at(r) * tps + t, ci)
                        for e in range(1, tps):
                            fwd_copy(i, r, ci, e).start()
            take(n, t)
        loop(chunks // group, across)

        def far(n):
            for e in range(1, tps):
                @pl.when(layer > 0)
                def _():
                    for m in range(group):
                        for r in range(1, SUBS):
                            wait_block(i, sub_at(r) * tps + tp_at(e), n * group + m)
                take(n, tp_at(e))
        loop(chunks // group, far)

        scale = lax.rsqrt(jnp.sum(sumsq[...], axis=1, keepdims=True) / depth + NORM_EPS)
        kv = kvacc[...]
        for r in range(1, SUBS):
            kvp_copy(i, r).wait_recv()
            kv = kv + kvrecv[i, r - 1].astype(F32)
        kv = kv * scale
        kvb[i + 1, :, :HEAD_DIM] = rotate(kv[:, :HEAD_DIM], i).astype(BF16)
        kvb[i + 1, :, HEAD_DIM:] = kv[:, HEAD_DIM:].astype(BF16)
        both = jnp.concatenate([kvb[i], kvb[i + 1]], axis=0)
        key_ids = (i - 1) * span + lax.broadcasted_iota(jnp.int32, (span, 2 * span), 1)
        query_ids = i * span + lax.broadcasted_iota(jnp.int32, (span, 2 * span), 0)
        allowed = (key_ids >= first[i]) & (key_ids <= query_ids)
        for g in range(att.shape[1] // HEAD_DIM):
            cols = slice(g * HEAD_DIM, (g + 1) * HEAD_DIM)
            query = rotate(qacc[:, cols] * scale, i).astype(BF16)
            scores = lax.dot_general(
                query, both[:, :HEAD_DIM], (((1,), (1,)), ((), ())), preferred_element_type=F32
            ) * (1.0 / math.sqrt(HEAD_DIM))
            weights = jnp.where(allowed, jnp.exp(scores), 0.0)
            probs = (weights / jnp.sum(weights, axis=1, keepdims=True)).astype(BF16)
            att[:, cols] = dot(probs, both[:, HEAD_DIM:]).astype(BF16)

        @pl.when(i == 0)
        def _():
            out_load.wait()

        def term(p, ci):
            cols = pl.ds(pl.multiple_of((p * chunks + ci) * block, block), block)
            return dot(att[...], wo[:, cols]).astype(BF16)

        def project(k):
            @pl.when(k < chunks)
            def _():
                for e in range(1, tps):
                    for r in (1, 2, 3, 0):
                        s1out[i, r, k, e - 1] = term(sub_at(r) * tps + tp_at(e), k)
                    for r in (1, 2, 3, 0):
                        s1_copy(i, r, k, e).start()
                for r in range(SUBS):
                    s1own[i, r, k] = term(sub_at(r) * tps + t, k)

            @pl.when(k >= 1)
            def _():
                ci = k - 1
                for r in (1, 2, 3, 0):
                    total = s1own[i, r, ci].astype(F32)
                    for e in range(1, tps):
                        s1_copy(i, r, ci, e).wait_recv()
                        total = total + s1in[i, r, ci, e - 1].astype(F32)
                    s1own[i, r, ci] = total.astype(BF16)
                    if r > 0:
                        s2_copy(i, r, ci).start()
        loop(chunks + 1, project)

        @pl.when(i == splits - 1)
        def _():
            def deliver(j):
                rows = dot(pick[j, 0], kvb[1])
                for n in range(1, splits):
                    rows = rows + dot(pick[j, n], kvb[n + 1])
                pickst[j] = rows.astype(BF16)

                @pl.when(j == layer)
                def _():
                    kvbuf[layer] = pickst[j]

                @pl.when(j != layer)
                def _():
                    pick_copy(j).start()
            loop(layers, deliver)

        def finish(ci):
            @pl.when(ci < chunks)
            def _():
                terms = s1own[i, 0, ci].astype(F32)
                for r in range(1, SUBS):
                    s2_copy(i, r, ci).wait_recv()
                    terms = terms + s2in[i, r - 1, ci].astype(F32)
                total = hbuf[i, own, ci].astype(F32) + terms

                @pl.when(layer < last)
                def _():
                    upd[i, ci] = total.astype(BF16)
                    z_copy(i, ci).start()

                @pl.when(layer == last)
                def _():
                    totf[:span] = total
                    for n in range(per_split):
                        rows = totf[n * own_tokens:n * own_tokens + fst.shape[2]]
                        fst[i * per_split + n, ci] = rows.astype(BF16)

            @pl.when((ci >= 1) & (layer > 0) & (i < splits - 1))
            def _():
                spread(i + 1, ci - 1)
        loop(chunks + 1, finish)

        @pl.when((layer == 0) & (i == 0))
        def _():
            loop(SUBS * chunks, send_rest)

        @pl.when(layer == last)
        def _():
            def out(n):
                s = i * per_split + n
                mine = (s == section) & (out_tp == t)

                @pl.when(mine)
                def _():
                    fin[out_slot] = fst[s]

                @pl.when(jnp.logical_not(mine))
                def _():
                    fin_copy(s).start()
            loop(per_split, out)

    loop(splits, stage)

    def kv_in(j):
        @pl.when(j != layer)
        def _():
            copy(pickst.at[j], kvbuf.at[j], pk_s.at[j], pk_r.at[j], j * SUBS + u, t).wait_recv()
    loop(layers, kv_in)
    kv_out[...] = kvbuf[...]

    def fin_in(j):
        p = t * SUBS + j
        sec, core = last * SUBS + p // tps, p % tps

        @pl.when((sec != section) | (core != t))
        def _():
            copy(fst.at[0], fin.at[j], fin_s.at[0], fin_r.at[j], sec, core).wait_recv()
    loop(SUBS, fin_in)
    fin_out[...] = fin[...]

    @pl.when(layer == 0)
    def _():
        def sent(k):
            for e in range(1, tps):
                first_copy(k // (SUBS * chunks), k // chunks % SUBS, k % chunks, e).wait_send()
        loop(splits * SUBS * chunks, sent)

    @pl.when(layer > 0)
    def _():
        def sent(k):
            i, ci = k // chunks, k % chunks
            for r in range(SUBS):
                for e in range(1, tps):
                    fwd_copy(i, r, ci, e).wait_send()
            for r in range(1, SUBS):
                ag_copy(i, r, ci).wait_send()
        loop(splits * chunks, sent)

    def kvp_sent(i):
        for r in range(1, SUBS):
            kvp_copy(i, r).wait_send()
    loop(splits, kvp_sent)

    def sums_sent(k):
        i, ci = k // chunks, k % chunks
        for r in range(SUBS):
            for e in range(1, tps):
                s1_copy(i, r, ci, e).wait_send()
        for r in range(1, SUBS):
            s2_copy(i, r, ci).wait_send()

        @pl.when(layer < last)
        def _():
            z_copy(i, ci).wait_send()
    loop(splits * chunks, sums_sent)

    def kv_sent(j):
        @pl.when(j != layer)
        def _():
            pick_copy(j).wait_send()
    loop(layers, kv_sent)

    @pl.when(layer == last)
    def _():
        def sent(s):
            @pl.when(jnp.logical_not((s == section) & (out_tp == t)))
            def _():
                fin_copy(s).wait_send()
        loop(sections, sent)


def shards(
    hidden_t, norm_gain, q_weight, k_weight, v_weight, o_weight, lengths, prior_offsets, owners
):
    sections = lax.axis_size("section")
    tps = lax.axis_size("tp")
    section = lax.axis_index("section")
    layers = sections // SUBS
    layer = section // SUBS
    sub = section % SUBS
    rows_dev, tokens = hidden_t.shape
    num_reqs = lengths.shape[0]
    capacity = 2 * tokens // num_reqs
    cap_pad = round_up(capacity, 16)
    own_tokens = tokens // sections
    tok_pad = round_up(own_tokens, 16)
    pieces = SUBS * tps
    block = min(BLOCK, rows_dev // SUBS)
    chunks = rows_dev // SUBS // block
    q_cols = q_weight.shape[2]
    span = tokens // SPLIT
    assert span >= capacity and sections % SPLIT == 0 and span % 16 == 0

    req_ends = jnp.cumsum(lengths)
    req_starts = req_ends - lengths
    tok_ids = jnp.arange(tokens, dtype=jnp.int32)
    req_ids = jnp.arange(num_reqs, dtype=jnp.int32)
    req_of_tok = jnp.sum((tok_ids[:, None] >= req_ends[None, :]).astype(jnp.int32), axis=1)
    req_onehot = req_of_tok[:, None] == req_ids[None, :]
    positions = (
        jnp.sum(jnp.where(req_onehot, (prior_offsets - req_starts)[None, :], 0), axis=1) + tok_ids
    )
    first = jnp.sum(jnp.where(req_onehot, req_starts[None, :], 0), axis=1).reshape(SPLIT, span, 1)
    half = HEAD_DIM // 2
    lanes = jnp.arange(HEAD_DIM, dtype=jnp.int32)
    inv_freq = jnp.power(F32(ROPE_BASE), -(2.0 * (lanes % half).astype(F32)) / HEAD_DIM)
    angle = positions.astype(F32).reshape(SPLIT, span, 1) * inv_freq
    cosf = jnp.cos(angle)
    sinf = jnp.sin(angle) * jnp.where(lanes < half, -1.0, 1.0)

    mine = jnp.arange(layers, dtype=jnp.int32) * SUBS + sub
    chosen = owners[None, :] == mine[:, None]
    start = jnp.sum(jnp.where(chosen, req_starts[None, :], 0), axis=1)
    count = jnp.sum(jnp.where(chosen, lengths[None, :], 0), axis=1)
    slots = jnp.arange(cap_pad, dtype=jnp.int32)
    tok_split = tok_ids.reshape(1, SPLIT, 1, span)
    slots = slots[None, None, :, None]
    pick = (
        (tok_split == start[:, None, None, None] + slots) & (slots < count[:, None, None, None])
    ).astype(BF16)

    gain = lax.dynamic_index_in_dim(norm_gain, layer, 0, keepdims=False).astype(F32)
    gain = gain.reshape(pieces * chunks, 1, block)

    vm = pltpu.VMEM
    dma = pltpu.SemaphoreType.DMA
    others = tps - 1
    far_subs = SUBS - 1
    blk = (span, block)
    kv_cols = 2 * HEAD_DIM
    fin, kv = pl.pallas_call(
        functools.partial(relay_kernel, layers, tps, own_tokens),
        out_shape=(
            jax.ShapeDtypeStruct((SUBS, chunks, tok_pad, block), BF16),
            jax.ShapeDtypeStruct((layers, cap_pad, 2 * HEAD_DIM), BF16),
        ),
        in_specs=[pl.BlockSpec(memory_space=pl.ANY)] * 5 + [pl.BlockSpec(memory_space=pltpu.VMEM)] * 5,
        out_specs=(pl.BlockSpec(memory_space=pltpu.VMEM),) * 2,
        scratch_shapes=[
            vm((SPLIT, pieces, chunks) + blk, BF16),
            vm((span, q_cols), F32),
            vm((span, kv_cols), F32),
            vm((span, HEAD_DIM), F32),
            vm((SPLIT, span, kv_cols), BF16),
            vm((SPLIT, far_subs, span, kv_cols), BF16),
            vm((SPLIT + 1, span, kv_cols), BF16),
            vm((span, q_cols), BF16),
            vm((SPLIT, SUBS, chunks, others) + blk, BF16),
            vm((SPLIT, SUBS, chunks, others) + blk, BF16),
            vm((SPLIT, SUBS, chunks) + blk, BF16),
            vm((SPLIT, far_subs, chunks) + blk, BF16),
            vm((SPLIT, chunks) + blk, BF16),
            vm((span + 32, block), F32),
            vm((sections, chunks, tok_pad, block), BF16),
            vm((SUBS, chunks, tok_pad, block), BF16),
            vm((layers, cap_pad, 2 * HEAD_DIM), BF16),
            vm((layers, cap_pad, 2 * HEAD_DIM), BF16),
            dma((SPLIT, pieces, chunks)),
            dma((SPLIT, SUBS, chunks, others)),
            dma((SPLIT, far_subs, chunks)),
            dma((SPLIT, far_subs)),
            dma((SPLIT, far_subs)),
            dma((SPLIT, SUBS, chunks, others)),
            dma((SPLIT, SUBS, chunks, others)),
            dma((SPLIT, far_subs, chunks)),
            dma((SPLIT, far_subs, chunks)),
            dma((SPLIT, chunks)),
            dma((layers,)),
            dma((layers,)),
            dma((sections,)),
            dma((SUBS,)),
            vm(hidden_t.shape, BF16),
            vm(q_weight.shape[1:], BF16),
            vm(k_weight.shape[1:], BF16),
            vm(v_weight.shape[1:], BF16),
            vm(o_weight.shape[1:], BF16),
            dma((5,)),
        ],
        compiler_params=pltpu.CompilerParams(
            collective_id=0, has_side_effects=True, vmem_limit_bytes=56 * 1024 * 1024
        ),
        name="relay",
    )(hidden_t, q_weight[0], k_weight[0], v_weight[0], o_weight[0], gain, cosf, sinf, first, pick)
    final_hidden = fin[:, :, :own_tokens].transpose(0, 1, 3, 2).reshape(rows_dev, own_tokens)
    return final_hidden, kv[None, :, :capacity]


def solution(mesh):
    return jax.shard_map(
        shards,
        mesh=mesh,
        in_specs=(
            P("tp", None),
            P(),
            P("section", None, "tp"),
            P("section", None, "tp"),
            P("section", None, "tp"),
            P("section", "tp", None),
            P(),
            P(),
            P(),
        ),
        out_specs=(P("tp", "section"), P("section", None, None, "tp")),
        check_vma=False,
    )
```

```python
import functools
import math

import jax
import jax.numpy as jnp
from jax import lax
from jax.experimental import pallas as pl
from jax.experimental.pallas import tpu as pltpu
from jax.sharding import PartitionSpec as P

HEAD_DIM = 128
SUBS = 4
BLOCK = 256
GROUP = 2
SPLIT = 4
NORM_EPS = 1e-05
ROPE_BASE = 500000.0
MESH = pl.DeviceIdType.MESH
F32 = jnp.float32
BF16 = jnp.bfloat16


def dot(a, b):
    return jnp.dot(a, b, preferred_element_type=F32)


def round_up(count, unit):
    return (count + unit - 1) // unit * unit


def relay_kernel(
    layers, tps, own_tokens,
    hin_hbm, wq_hbm, wk_hbm, wv_hbm, wo_hbm, gain, cosf, sinf, first, pick,
    fin_out, kv_out,
    hbuf, qacc, kvacc, sumsq, kvst, kvrecv, kvb, att,
    s1out, s1in, s1own, s2in, upd, totf, fst, fin, pickst, kvbuf,
    hs, fwd_s, ag_s, kvp_s, kvp_r, s1_s, s1_r, s2_s, s2_r, z_s, pk_s, pk_r, fin_s, fin_r,
    hin, wq, wk, wv, wo, load_s,
):
    section = lax.axis_index("section")
    t = lax.axis_index("tp")
    layer = section // SUBS
    u = section % SUBS
    splits, pieces, chunks, span, block = hbuf.shape
    depth = pieces * chunks * block
    group = min(GROUP, chunks)
    per_split = layers * SUBS // splits
    own = u * tps + t
    sections = layers * SUBS
    last = layers - 1
    out_tp = own // SUBS
    out_slot = own % SUBS
    base = layer * SUBS

    def copy(src, dst, send, recv, sec, core):
        return pltpu.make_async_remote_copy(
            src_ref=src, dst_ref=dst, send_sem=send, recv_sem=recv,
            device_id=(sec, core), device_id_type=MESH,
        )

    def sub_at(r):
        return (u + r) % SUBS

    def tp_at(e):
        return (t + e) % tps

    def first_copy(i, j, ci, e):
        p = t * SUBS + j
        return copy(hbuf.at[i, p, ci], hbuf.at[i, p, ci], fwd_s.at[i, j, ci, e - 1], hs.at[i, p, ci],
                    section, tp_at(e))

    def fwd_copy(i, r, ci, e):
        p = sub_at(r) * tps + t
        return copy(hbuf.at[i, p, ci], hbuf.at[i, p, ci], fwd_s.at[i, r, ci, e - 1], hs.at[i, p, ci],
                    section, tp_at(e))

    def ag_copy(i, r, ci):
        return copy(hbuf.at[i, own, ci], hbuf.at[i, own, ci], ag_s.at[i, r - 1, ci], hs.at[i, own, ci],
                    base + sub_at(r), t)

    def wait_block(i, p, ci):
        copy(hbuf.at[i, p, ci], hbuf.at[i, p, ci], fwd_s.at[0, 0, 0, 0], hs.at[i, p, ci],
             section, tp_at(1)).wait_recv()

    def kvp_copy(i, r):
        return copy(kvst.at[i], kvrecv.at[i, r - 1], kvp_s.at[i, r - 1], kvp_r.at[i, r - 1],
                    base + sub_at(r), t)

    def s1_copy(i, r, ci, e):
        return copy(s1out.at[i, r, ci, e - 1], s1in.at[i, r, ci, e - 1], s1_s.at[i, r, ci, e - 1],
                    s1_r.at[i, r, ci, e - 1], section, tp_at(e))

    def s2_copy(i, r, ci):
        return copy(s1own.at[i, r, ci], s2in.at[i, r - 1, ci], s2_s.at[i, r - 1, ci], s2_r.at[i, r - 1, ci],
                    base + sub_at(r), t)

    def z_copy(i, ci):
        return copy(upd.at[i, ci], hbuf.at[i, own, ci], z_s.at[i, ci], hs.at[i, own, ci], section + SUBS, t)

    def pick_copy(j):
        return copy(pickst.at[j], kvbuf.at[layer], pk_s.at[j], pk_r.at[layer], j * SUBS + u, t)

    def fin_copy(s):
        return copy(fst.at[s], fin.at[out_slot], fin_s.at[s], fin_r.at[out_slot], s, out_tp)

    def loop(count, body):
        def step(k, carry):
            body(k)
            return carry
        lax.fori_loop(0, count, step, jnp.int32(0))

    def load(n, src, dst):
        return pltpu.make_async_copy(src, dst, load_s.at[n])

    in_load = load(0, hin_hbm, hin)
    out_load = load(4, wo_hbm, wo)
    loads = (load(1, wq_hbm, wq), load(2, wk_hbm, wk), load(3, wv_hbm, wv))

    @pl.when(layer == 0)
    def _():
        in_load.start()
    for each in loads:
        each.start()
    out_load.start()

    barrier = pltpu.get_barrier_semaphore()

    def greet(sec, core):
        pl.semaphore_signal(barrier, inc=1, device_id=(sec, core), device_id_type=MESH)

    for e in range(1, tps):
        greet(section, tp_at(e))
    for r in range(1, SUBS):
        greet(base + sub_at(r), t)
    for j in range(1, layers):
        greet((layer + j) % layers * SUBS + u, t)
    for j in range(SUBS):
        p = t * SUBS + j
        sec, core = last * SUBS + p // tps, p % tps

        @pl.when((sec != section) | (core != t))
        def _():
            greet(sec, core)

    spread_to = jnp.where(layer == last, sections - jnp.where(out_tp == t, 1, 0), 0)
    pl.semaphore_wait(barrier, (tps - 1) + (SUBS - 1) + (layers - 1) + spread_to)

    totf[...] = jnp.zeros_like(totf)
    kvb[0] = jnp.zeros_like(kvb[0])

    @pl.when(layer == 0)
    def _():
        in_load.wait()
        wide = round_up(span, HEAD_DIM)

        def send(k):
            j, ci = k // chunks, k % chunks
            rows = pl.ds(pl.multiple_of(k * block, block), block)
            turned = hin[rows, :wide].astype(F32).T.astype(BF16)
            hbuf[0, t * SUBS + j, ci] = turned[:span]
            for e in range(1, tps):
                first_copy(0, j, ci, e).start()
        loop(SUBS * chunks, send)

    def send_rest(k):
        j, ci = k // chunks, k % chunks
        rows = pl.ds(pl.multiple_of(k * block, block), block)
        turned = hin[rows, :].astype(F32).T.astype(BF16)
        for i in range(1, splits):
            hbuf[i, t * SUBS + j, ci] = turned[i * span:(i + 1) * span]
            for e in range(1, tps):
                first_copy(i, j, ci, e).start()

    for each in loads:
        each.wait()

    def spread(i, ci):
        wait_block(i, own, ci)
        for r in range(1, SUBS):
            ag_copy(i, r, ci).start()
        for e in range(1, tps):
            fwd_copy(i, 0, ci, e).start()

    def rotate(x, i):
        return x * cosf[i] + pltpu.roll(x, HEAD_DIM // 2, 1) * sinf[i]

    def stage(i):
        qacc[...] = jnp.zeros_like(qacc)
        kvacc[...] = jnp.zeros_like(kvacc)
        sumsq[...] = jnp.zeros_like(sumsq)

        @pl.when(layer == 0)
        def _():
            def arrive(k):
                j, ci = k // chunks, k % chunks
                for e in range(1, tps):
                    wait_block(i, tp_at(e) * SUBS + j, ci)
            loop(SUBS * chunks, arrive)

        @pl.when((layer > 0) & (i == 0))
        def _():
            loop(chunks, lambda ci: spread(0, ci))

        def absorb(p, n):
            parts, squares = [], 0.0
            for m in range(group):
                ci = n * group + m
                x = hbuf[i, p, ci].astype(F32)
                sq = x * x
                for w in range(block // HEAD_DIM):
                    squares = squares + sq[:, w * HEAD_DIM:(w + 1) * HEAD_DIM]
                parts.append((x * gain[p * chunks + ci]).astype(BF16))
            scaled = jnp.concatenate(parts, axis=1)
            width = group * block
            rows = pl.ds(pl.multiple_of(p * chunks * block + n * width, width), width)
            return scaled, dot(scaled, wq[rows, :]), squares

        def near(n):
            for m in range(group):
                for e in range(1, tps):
                    @pl.when(layer > 0)
                    def _():
                        wait_block(i, u * tps + tp_at(e), n * group + m)
            query_sum, square_sum, kv_sum = 0.0, 0.0, 0.0
            width = group * block
            for e in range(tps):
                d = tp_at(e)
                scaled, query, squares = absorb(u * tps + d, n)
                query_sum, square_sum = query_sum + query, square_sum + squares
                rows = pl.ds(pl.multiple_of(d * chunks * block + n * width, width), width)
                kv_sum = kv_sum + dot(scaled, jnp.concatenate([wk[rows, :], wv[rows, :]], axis=1))
            qacc[...] += query_sum
            sumsq[...] += square_sum
            kvacc[...] += kv_sum
        loop(chunks // group, near)

        kvst[i] = kvacc[...].astype(BF16)
        for r in range(1, SUBS):
            kvp_copy(i, r).start()

        def take(n, core):
            query_sum, square_sum = 0.0, 0.0
            for r in range(1, SUBS):
                scaled, query, squares = absorb(sub_at(r) * tps + core, n)
                query_sum, square_sum = query_sum + query, square_sum + squares
            qacc[...] += query_sum
            sumsq[...] += square_sum

        def across(n):
            @pl.when(layer > 0)
            def _():
                for m in range(group):
                    for r in range(1, SUBS):
                        ci = n * group + m
                        wait_block(i, sub_at(r) * tps + t, ci)
                        for e in range(1, tps):
                            fwd_copy(i, r, ci, e).start()
            take(n, t)
        loop(chunks // group, across)

        def far(n):
            for e in range(1, tps):
                @pl.when(layer > 0)
                def _():
                    for m in range(group):
                        for r in range(1, SUBS):
                            wait_block(i, sub_at(r) * tps + tp_at(e), n * group + m)
                take(n, tp_at(e))
        loop(chunks // group, far)

        scale = lax.rsqrt(jnp.sum(sumsq[...], axis=1, keepdims=True) / depth + NORM_EPS)
        kv = kvacc[...]
        for r in range(1, SUBS):
            kvp_copy(i, r).wait_recv()
            kv = kv + kvrecv[i, r - 1].astype(F32)
        kv = kv * scale
        kvb[i + 1, :, :HEAD_DIM] = rotate(kv[:, :HEAD_DIM], i).astype(BF16)
        kvb[i + 1, :, HEAD_DIM:] = kv[:, HEAD_DIM:].astype(BF16)
        both = jnp.concatenate([kvb[i], kvb[i + 1]], axis=0)
        key_ids = (i - 1) * span + lax.broadcasted_iota(jnp.int32, (span, 2 * span), 1)
        query_ids = i * span + lax.broadcasted_iota(jnp.int32, (span, 2 * span), 0)
        allowed = (key_ids >= first[i]) & (key_ids <= query_ids)
        for g in range(att.shape[1] // HEAD_DIM):
            cols = slice(g * HEAD_DIM, (g + 1) * HEAD_DIM)
            query = rotate(qacc[:, cols] * scale, i).astype(BF16)
            scores = lax.dot_general(
                query, both[:, :HEAD_DIM], (((1,), (1,)), ((), ())), preferred_element_type=F32
            ) * (1.0 / math.sqrt(HEAD_DIM))
            weights = jnp.where(allowed, jnp.exp(scores), 0.0)
            probs = (weights / jnp.sum(weights, axis=1, keepdims=True)).astype(BF16)
            att[:, cols] = dot(probs, both[:, HEAD_DIM:]).astype(BF16)

        @pl.when(i == 0)
        def _():
            out_load.wait()

        def term(p, ci):
            cols = pl.ds(pl.multiple_of((p * chunks + ci) * block, block), block)
            return dot(att[...], wo[:, cols]).astype(BF16)

        def project(k):
            @pl.when(k >= 1)
            def _():
                ci = k - 1
                for r in (1, 2, 3, 0):
                    total = s1own[i, r, ci].astype(F32)
                    for e in range(1, tps):
                        s1_copy(i, r, ci, e).wait_recv()
                        total = total + s1in[i, r, ci, e - 1].astype(F32)
                    s1own[i, r, ci] = total.astype(BF16)
                    if r > 0:
                        s2_copy(i, r, ci).start()

            @pl.when(k < chunks)
            def _():
                for e in range(1, tps):
                    for r in (1, 2, 3, 0):
                        s1out[i, r, k, e - 1] = term(sub_at(r) * tps + tp_at(e), k)
                    for r in (1, 2, 3, 0):
                        s1_copy(i, r, k, e).start()
                for r in range(SUBS):
                    s1own[i, r, k] = term(sub_at(r) * tps + t, k)
        loop(chunks + 1, project)

        @pl.when(i == splits - 1)
        def _():
            def deliver(j):
                rows = dot(pick[j, 0], kvb[1])
                for n in range(1, splits):
                    rows = rows + dot(pick[j, n], kvb[n + 1])
                pickst[j] = rows.astype(BF16)

                @pl.when(j == layer)
                def _():
                    kvbuf[layer] = pickst[j]

                @pl.when(j != layer)
                def _():
                    pick_copy(j).start()
            loop(layers, deliver)

        def finish(ci):
            @pl.when(ci < chunks)
            def _():
                terms = s1own[i, 0, ci].astype(F32)
                for r in range(1, SUBS):
                    s2_copy(i, r, ci).wait_recv()
                    terms = terms + s2in[i, r - 1, ci].astype(F32)
                total = hbuf[i, own, ci].astype(F32) + terms

                @pl.when(layer < last)
                def _():
                    upd[i, ci] = total.astype(BF16)
                    z_copy(i, ci).start()

                @pl.when(layer == last)
                def _():
                    totf[:span] = total
                    for n in range(per_split):
                        rows = totf[n * own_tokens:n * own_tokens + fst.shape[2]]
                        fst[i * per_split + n, ci] = rows.astype(BF16)

            @pl.when((ci >= 1) & (layer > 0) & (i < splits - 1))
            def _():
                spread(i + 1, ci - 1)
        loop(chunks + 1, finish)

        @pl.when((layer == 0) & (i == 0))
        def _():
            loop(SUBS * chunks, send_rest)

        @pl.when(layer == last)
        def _():
            def out(n):
                s = i * per_split + n
                mine = (s == section) & (out_tp == t)

                @pl.when(mine)
                def _():
                    fin[out_slot] = fst[s]

                @pl.when(jnp.logical_not(mine))
                def _():
                    fin_copy(s).start()
            loop(per_split, out)

    loop(splits, stage)

    def kv_in(j):
        @pl.when(j != layer)
        def _():
            copy(pickst.at[j], kvbuf.at[j], pk_s.at[j], pk_r.at[j], j * SUBS + u, t).wait_recv()
    loop(layers, kv_in)
    kv_out[...] = kvbuf[...]

    def fin_in(j):
        p = t * SUBS + j
        sec, core = last * SUBS + p // tps, p % tps

        @pl.when((sec != section) | (core != t))
        def _():
            copy(fst.at[0], fin.at[j], fin_s.at[0], fin_r.at[j], sec, core).wait_recv()
    loop(SUBS, fin_in)
    fin_out[...] = fin[...]

    @pl.when(layer == 0)
    def _():
        def sent(k):
            for e in range(1, tps):
                first_copy(k // (SUBS * chunks), k // chunks % SUBS, k % chunks, e).wait_send()
        loop(splits * SUBS * chunks, sent)

    @pl.when(layer > 0)
    def _():
        def sent(k):
            i, ci = k // chunks, k % chunks
            for r in range(SUBS):
                for e in range(1, tps):
                    fwd_copy(i, r, ci, e).wait_send()
            for r in range(1, SUBS):
                ag_copy(i, r, ci).wait_send()
        loop(splits * chunks, sent)

    def kvp_sent(i):
        for r in range(1, SUBS):
            kvp_copy(i, r).wait_send()
    loop(splits, kvp_sent)

    def sums_sent(k):
        i, ci = k // chunks, k % chunks
        for r in range(SUBS):
            for e in range(1, tps):
                s1_copy(i, r, ci, e).wait_send()
        for r in range(1, SUBS):
            s2_copy(i, r, ci).wait_send()

        @pl.when(layer < last)
        def _():
            z_copy(i, ci).wait_send()
    loop(splits * chunks, sums_sent)

    def kv_sent(j):
        @pl.when(j != layer)
        def _():
            pick_copy(j).wait_send()
    loop(layers, kv_sent)

    @pl.when(layer == last)
    def _():
        def sent(s):
            @pl.when(jnp.logical_not((s == section) & (out_tp == t)))
            def _():
                fin_copy(s).wait_send()
        loop(sections, sent)


def shards(
    hidden_t, norm_gain, q_weight, k_weight, v_weight, o_weight, lengths, prior_offsets, owners
):
    sections = lax.axis_size("section")
    tps = lax.axis_size("tp")
    section = lax.axis_index("section")
    layers = sections // SUBS
    layer = section // SUBS
    sub = section % SUBS
    rows_dev, tokens = hidden_t.shape
    num_reqs = lengths.shape[0]
    capacity = 2 * tokens // num_reqs
    cap_pad = round_up(capacity, 16)
    own_tokens = tokens // sections
    tok_pad = round_up(own_tokens, 16)
    pieces = SUBS * tps
    block = min(BLOCK, rows_dev // SUBS)
    chunks = rows_dev // SUBS // block
    q_cols = q_weight.shape[2]
    span = tokens // SPLIT
    assert span >= capacity and sections % SPLIT == 0 and span % 16 == 0

    req_ends = jnp.cumsum(lengths)
    req_starts = req_ends - lengths
    tok_ids = jnp.arange(tokens, dtype=jnp.int32)
    req_ids = jnp.arange(num_reqs, dtype=jnp.int32)
    req_of_tok = jnp.sum((tok_ids[:, None] >= req_ends[None, :]).astype(jnp.int32), axis=1)
    req_onehot = req_of_tok[:, None] == req_ids[None, :]
    positions = (
        jnp.sum(jnp.where(req_onehot, (prior_offsets - req_starts)[None, :], 0), axis=1) + tok_ids
    )
    first = jnp.sum(jnp.where(req_onehot, req_starts[None, :], 0), axis=1).reshape(SPLIT, span, 1)
    half = HEAD_DIM // 2
    lanes = jnp.arange(HEAD_DIM, dtype=jnp.int32)
    inv_freq = jnp.power(F32(ROPE_BASE), -(2.0 * (lanes % half).astype(F32)) / HEAD_DIM)
    angle = positions.astype(F32).reshape(SPLIT, span, 1) * inv_freq
    cosf = jnp.cos(angle)
    sinf = jnp.sin(angle) * jnp.where(lanes < half, -1.0, 1.0)

    mine = jnp.arange(layers, dtype=jnp.int32) * SUBS + sub
    chosen = owners[None, :] == mine[:, None]
    start = jnp.sum(jnp.where(chosen, req_starts[None, :], 0), axis=1)
    count = jnp.sum(jnp.where(chosen, lengths[None, :], 0), axis=1)
    slots = jnp.arange(cap_pad, dtype=jnp.int32)
    tok_split = tok_ids.reshape(1, SPLIT, 1, span)
    slots = slots[None, None, :, None]
    pick = (
        (tok_split == start[:, None, None, None] + slots) & (slots < count[:, None, None, None])
    ).astype(BF16)

    gain = lax.dynamic_index_in_dim(norm_gain, layer, 0, keepdims=False).astype(F32)
    gain = gain.reshape(pieces * chunks, 1, block)

    vm = pltpu.VMEM
    dma = pltpu.SemaphoreType.DMA
    others = tps - 1
    far_subs = SUBS - 1
    blk = (span, block)
    kv_cols = 2 * HEAD_DIM
    fin, kv = pl.pallas_call(
        functools.partial(relay_kernel, layers, tps, own_tokens),
        out_shape=(
            jax.ShapeDtypeStruct((SUBS, chunks, tok_pad, block), BF16),
            jax.ShapeDtypeStruct((layers, cap_pad, 2 * HEAD_DIM), BF16),
        ),
        in_specs=[pl.BlockSpec(memory_space=pl.ANY)] * 5 + [pl.BlockSpec(memory_space=pltpu.VMEM)] * 5,
        out_specs=(pl.BlockSpec(memory_space=pltpu.VMEM),) * 2,
        scratch_shapes=[
            vm((SPLIT, pieces, chunks) + blk, BF16),
            vm((span, q_cols), F32),
            vm((span, kv_cols), F32),
            vm((span, HEAD_DIM), F32),
            vm((SPLIT, span, kv_cols), BF16),
            vm((SPLIT, far_subs, span, kv_cols), BF16),
            vm((SPLIT + 1, span, kv_cols), BF16),
            vm((span, q_cols), BF16),
            vm((SPLIT, SUBS, chunks, others) + blk, BF16),
            vm((SPLIT, SUBS, chunks, others) + blk, BF16),
            vm((SPLIT, SUBS, chunks) + blk, BF16),
            vm((SPLIT, far_subs, chunks) + blk, BF16),
            vm((SPLIT, chunks) + blk, BF16),
            vm((span + 32, block), F32),
            vm((sections, chunks, tok_pad, block), BF16),
            vm((SUBS, chunks, tok_pad, block), BF16),
            vm((layers, cap_pad, 2 * HEAD_DIM), BF16),
            vm((layers, cap_pad, 2 * HEAD_DIM), BF16),
            dma((SPLIT, pieces, chunks)),
            dma((SPLIT, SUBS, chunks, others)),
            dma((SPLIT, far_subs, chunks)),
            dma((SPLIT, far_subs)),
            dma((SPLIT, far_subs)),
            dma((SPLIT, SUBS, chunks, others)),
            dma((SPLIT, SUBS, chunks, others)),
            dma((SPLIT, far_subs, chunks)),
            dma((SPLIT, far_subs, chunks)),
            dma((SPLIT, chunks)),
            dma((layers,)),
            dma((layers,)),
            dma((sections,)),
            dma((SUBS,)),
            vm(hidden_t.shape, BF16),
            vm(q_weight.shape[1:], BF16),
            vm(k_weight.shape[1:], BF16),
            vm(v_weight.shape[1:], BF16),
            vm(o_weight.shape[1:], BF16),
            dma((5,)),
        ],
        compiler_params=pltpu.CompilerParams(
            collective_id=0, has_side_effects=True, vmem_limit_bytes=56 * 1024 * 1024
        ),
        name="relay",
    )(hidden_t, q_weight[0], k_weight[0], v_weight[0], o_weight[0], gain, cosf, sinf, first, pick)
    final_hidden = fin[:, :, :own_tokens].transpose(0, 1, 3, 2).reshape(rows_dev, own_tokens)
    return final_hidden, kv[None, :, :capacity]


def solution(mesh):
    return jax.shard_map(
        shards,
        mesh=mesh,
        in_specs=(
            P("tp", None),
            P(),
            P("section", None, "tp"),
            P("section", None, "tp"),
            P("section", None, "tp"),
            P("section", "tp", None),
            P(),
            P(),
            P(),
        ),
        out_specs=(P("tp", "section"), P("section", None, None, "tp")),
        check_vma=False,
    )
```
